128 devices in a mesh: gx: 4 (over y), gy: 32 (over x, z, core).
Axes of the slice: x: 4, y: 4, z: 4, core: 2. Of those that a mesh axis runs over, the one named last changes fastest.
Arguments:
- state: float32 [128, 1024, 256], P('gx', 'gy'), may hold values from -6 to 6
- group_member: int32 [131072, 1], P(('gx', 'gy')), may hold values from 0 to 127; in each aligned block of 1024 rows (0 to 1023, 1024 to 2047, ...) at most 16 rows name the same one
- w_in: bfloat16 [128, 256, 1024], P(('gx', 'gy')), may hold values from -0.375 to 0.375
- bias_in: float32 [128, 1024], P(('gx', 'gy')), may hold values from -3 to 3
- w_mid: bfloat16 [128, 1024, 1024], P(('gx', 'gy')), may hold values from -0.1875 to 0.1875
- bias_mid: float32 [128, 1024], P(('gx', 'gy')), may hold values from -3 to 3
- w_out: bfloat16 [128, 1024, 264], P(('gx', 'gy')), may hold values from -0.1875 to 0.1875
- intersection_element: int32 [16384], P(('gx', 'gy')), may hold values from 0 to 63
- ocean_owner: int32 [16384, 1], P(('gx', 'gy')), may hold values from 0 to 127; in each aligned block of 128 rows (0 to 127, 128 to 255, ...) at most 2 rows name the same one
- ocean_block: int32 [16384], P(('gx', 'gy')), may hold values from 0 to 15
- regrid_weight: float32 [16384, 256], P(('gx', 'gy')), may hold values from 0 to 0.25
Outputs:
- new_state: float32 [128, 1024, 256], P('gx', 'gy')
- ocean_flux: float32 [2048, 128], P(('gx', 'gy'))
The draws below stay inside these ranges and needn't reach their ends.
Inputs may be any that keep to these rules, and one draw needn't show every extreme that they name: `group_member`: in the columns of one device no member is named more than 16 times, and exactly 16 times for some member. `ocean_owner`: among the intersections of one device no owner is named more than 2 times, and exactly 2 times for some owner.
All inputs are finite; a program needn't handle non-finite values.
Results may differ from the reference program's by a relative error of at most 0.0046.
Values may be sent and summed in bfloat16 or wider, within the bound.
No kernel may reach another device: no remote copies, remote signals or barrier semaphores. Data moves between devices by JAX's collectives and lax.ppermute only.
A program may use at most 64 MiB of HBM per device.

```python
import math
import jax
import jax.numpy as jnp
import numpy as np
from jax import lax

LEV = 64
HID = 1024
NFLUX = 8
OCELL = 16
EL_X = 8
EL_Y = 8
LIST_DEV = 128
OB_DEV = 16
FEAT = 256
ABLK = 64
COLS_DEV = 1024
NXN = 128
NYN = 1024
COLUMNS = 131072
MEMBERS = 128
CAP = 16
OCAP = 2
INTERSECTIONS = 16384
NOB = 2048
N_GX = 4
N_GY = 32
DEVICES = 128


def touch_ends(values, own_key, low, top_value):
    place = [jax.random.randint(jax.random.fold_in(own_key, axis), (), 0, length) for axis, length in enumerate(values.shape)]
    widest = values.shape.index(max(values.shape))
    neighbour = place[:widest] + [(place[widest] + 1) % values.shape[widest]] + place[widest + 1:]
    return values.at[tuple(place)].set(low).at[tuple(neighbour)].set(top_value)


def steps_of(rng, dims, cuts, least, largest):
    def one(position, blocks):
        draws = jax.random.uniform(jax.random.fold_in(jax.random.fold_in(rng, 6), position), (blocks,), jnp.float32, least / len(cuts), largest / len(cuts))
        return jnp.repeat(jnp.exp(draws), dims[position] // blocks).reshape((-1,) + (1,) * (len(dims) - position - 1))

    factor_of = one(*cuts[0])
    for cut in cuts[1:]:
        factor_of = factor_of * one(*cut)
    return factor_of


def assign_block(stream_key, own, number, rows, count, top, most, lean):
    sequence = jax.random.permutation(stream_key, count)
    packed, common = load_shares(count, rows * top, most, lean, True), load_shares(count, rows * top, most, lean, False)
    places = jnp.arange(count)

    def named(sizes, offset_by):
        used = int((sizes > 0).sum())
        fixed = max(1, used // 4)
        passed = fixed + (places - fixed + offset_by * (used - fixed)) % max(1, count - fixed)
        return jnp.zeros((count,), jnp.int32).at[sequence[jnp.where(places < fixed, places, passed)]].set(jnp.asarray(sizes, jnp.int32))

    sizes = jnp.where(number % 4 == 0, named(packed, number // 4), named(common, number - number // 4 - 1))
    mixed = jax.random.permutation(jax.random.fold_in(own, 3), count)
    source_of, taker = mixed[0:count // 2 * 2:2], mixed[1:count // 2 * 2:2]
    margin = jnp.minimum(sizes[source_of] - 1, most - sizes[taker]) // 2
    margin = jnp.where((source_of == sequence[0]) | (taker == sequence[0]) | (sizes[taker] == 0), 0, jnp.maximum(margin, 0))
    passed = jax.random.randint(jax.random.fold_in(own, 4), (count // 2,), 0, 1 << 20) % (margin + 1)
    sizes = sizes.at[source_of].add(-passed).at[taker].add(passed)
    labels = jnp.searchsorted(jnp.cumsum(sizes), jnp.arange(rows * top), side="right").astype(jnp.int32)
    table = labels.reshape(top, rows).T
    table = table[jax.random.permutation(jax.random.fold_in(own, 1), rows)]
    offset_by = jax.random.randint(jax.random.fold_in(own, 2), (rows, 1), 0, top)
    return jnp.take_along_axis(table, (jnp.arange(top)[None, :] + offset_by) % top, axis=1)


def load_shares(amount, total, most, slope, full):
    portions = [(1 << 20) // math.isqrt(rank ** slope) + 1 for rank in range(1, amount + 1)]
    largest = most if full else min(most, max(-(-total // amount), total * portions[0] // sum(portions)))
    least = 1 if total - largest >= amount - 1 else 0
    holding, rest = [largest] + [least] * (amount - 1), total - largest - least * (amount - 1)
    while rest > 0:
        free = [i for i in range(1, amount) if holding[i] < largest] or [i for i in range(1, amount) if holding[i] < most]
        pool, remaining = sum([portions[i] for i in free]), rest
        for i in free:
            addition = min(most - holding[i], max(1, remaining * portions[i] // pool), rest)
            holding[i] = holding[i] + addition
            rest = rest - addition
    return np.array(holding)


def scatter_about(key, extent, width, most, pieces=(), kind=jnp.bfloat16):
    values = width * jax.random.normal(key, extent, jnp.float32)
    if pieces:
        values = values * steps_of(key, extent, pieces, -0.22, 0.18)
    return jnp.clip(values, -most, most).astype(kind)


def setup_inputs(seed: int = 0) -> dict:
    arg_keys = jax.random.split(jax.random.key(seed), 12)
    state = scatter_about(arg_keys[0], (NXN, NYN, FEAT), 1.0, 6.0, ((0, 4), (1, 32)), jnp.float32)
    group_member_keys = jax.random.split(jax.random.fold_in(arg_keys[1], 1), COLUMNS // COLS_DEV)
    group_member_turns = jax.random.permutation(jax.random.fold_in(arg_keys[1], 3), COLUMNS // COLS_DEV)
    group_member = jax.vmap(lambda own, number: assign_block(jax.random.fold_in(arg_keys[1], 2), own, number, COLS_DEV, MEMBERS, 1, CAP, 2))(group_member_keys, group_member_turns).reshape((COLUMNS, 1))
    w_in = scatter_about(arg_keys[2], (MEMBERS, FEAT, HID), FEAT ** -0.5, 0.375, ((0, 128),))
    bias_in = scatter_about(arg_keys[3], (MEMBERS, HID), 0.5, 3.0, ((0, 128),), jnp.float32)
    w_mid = scatter_about(arg_keys[4], (MEMBERS, HID, HID), HID ** -0.5, 0.1875, ((0, 128),))
    bias_mid = scatter_about(arg_keys[5], (MEMBERS, HID), 0.5, 3.0, ((0, 128),), jnp.float32)
    w_out = scatter_about(arg_keys[6], (MEMBERS, HID, FEAT + NFLUX), HID ** -0.5, 0.1875, ((0, 128),))
    intersection_element = touch_ends(jax.random.randint(arg_keys[7], (INTERSECTIONS,), 0, ABLK), jax.random.fold_in(arg_keys[7], 1), 0, ABLK - 1).astype(jnp.int32)
    ocean_owner_keys = jax.random.split(jax.random.fold_in(arg_keys[8], 1), INTERSECTIONS // LIST_DEV)
    ocean_owner_turns = jax.random.permutation(jax.random.fold_in(arg_keys[8], 3), INTERSECTIONS // LIST_DEV)
    ocean_owner = jax.vmap(lambda own, number: assign_block(jax.random.fold_in(arg_keys[8], 2), own, number, LIST_DEV, DEVICES, 1, OCAP, 2))(ocean_owner_keys, ocean_owner_turns).reshape((INTERSECTIONS, 1))
    ocean_block = touch_ends(jax.random.randint(arg_keys[9], (INTERSECTIONS,), 0, OB_DEV), jax.random.fold_in(arg_keys[9], 1), 0, OB_DEV - 1).astype(jnp.int32)
    regrid_weight = jnp.clip(0.25 * jax.random.uniform(arg_keys[10], (INTERSECTIONS, 16 * OCELL), jnp.float32) ** steps_of(arg_keys[10], (INTERSECTIONS, 16 * OCELL), ((0, 128),), -0.2, 0.2), 0.0, 0.25)
    return dict(state=state, group_member=group_member, w_in=w_in, bias_in=bias_in, w_mid=w_mid, bias_mid=bias_mid, w_out=w_out, intersection_element=intersection_element, ocean_owner=ocean_owner, ocean_block=ocean_block, regrid_weight=regrid_weight)


STEP_DT = 0.2
HIGHEST = lax.Precision.HIGHEST

def derivative_table():
    root = 1.0 / math.sqrt(5.0)
    nodes = np.array([-1.0, -root, root, 1.0])
    table = np.zeros((4, 4))
    for row_index in range(4):
        for col_index in range(4):
            if row_index == col_index:
                table[row_index, col_index] = sum((1.0 / (nodes[row_index] - nodes[other]) for other in range(4) if other != row_index))
            else:
                weight_row = np.prod([nodes[row_index] - nodes[other] for other in range(4) if other != row_index])
                weight_col = np.prod([nodes[col_index] - nodes[other] for other in range(4) if other != col_index])
                table[row_index, col_index] = weight_row / (weight_col * (nodes[row_index] - nodes[col_index]))
    return table

def element_tendency(field, deriv_table, levels):
    size_x, size_y, features = field.shape
    along_x = jnp.einsum('ij,ejyf->eiyf', deriv_table, field.reshape(size_x // 4, 4, size_y, features), precision=HIGHEST)
    along_y = jnp.einsum('ij,xejf->xeif', deriv_table, field.reshape(size_x, size_y // 4, 4, features), precision=HIGHEST)
    grid = field.reshape(size_x, size_y, 4, levels)
    wind_u = grid[:, :, 2:3, :]
    wind_v = grid[:, :, 3:4, :]
    tendency = -(wind_u * along_x.reshape(size_x, size_y, 4, levels) + wind_v * along_y.reshape(size_x, size_y, 4, levels))
    return tendency.reshape(size_x, size_y, features)

def stiffness_average(field):
    phase_x = (jnp.arange(field.shape[0]) % 4)[:, None, None]
    field = jnp.where(phase_x == 0, 0.5 * (field + jnp.roll(field, 1, 0)), jnp.where(phase_x == 3, 0.5 * (field + jnp.roll(field, -1, 0)), field))
    phase_y = (jnp.arange(field.shape[1]) % 4)[None, :, None]
    field = jnp.where(phase_y == 0, 0.5 * (field + jnp.roll(field, 1, 1)), jnp.where(phase_y == 3, 0.5 * (field + jnp.roll(field, -1, 1)), field))
    return field

def run_member(flat_rows, w_first, b_first, w_second, b_second, w_last):
    hidden_one = jax.nn.silu(jnp.dot(flat_rows.astype(jnp.float32), w_first.astype(jnp.float32)) + b_first).astype(jnp.bfloat16)
    hidden_two = jax.nn.silu(jnp.dot(hidden_one.astype(jnp.float32), w_second.astype(jnp.float32)) + b_second).astype(jnp.bfloat16)
    return jnp.dot(hidden_two.astype(jnp.float32), w_last.astype(jnp.float32)).astype(jnp.bfloat16)

def reference(state, group_member, w_in, bias_in, w_mid, bias_mid, w_out, intersection_element, ocean_owner, ocean_block, regrid_weight):
    deriv_table = jnp.asarray(derivative_table(), dtype=jnp.float32)
    tendency = element_tendency(state, deriv_table, LEV)
    advanced = state + STEP_DT * stiffness_average(tendency)
    local_x = 4 * EL_X
    local_y = 4 * EL_Y
    grid_cols = advanced.reshape(N_GX, local_x, N_GY, local_y, FEAT).transpose(0, 2, 1, 3, 4).reshape(COLUMNS, FEAT)
    columns = grid_cols.astype(jnp.bfloat16)
    padded_cols = jnp.concatenate([columns, jnp.zeros((1, FEAT), jnp.bfloat16)], axis=0)
    member_ids = group_member[:, 0]
    limit = MEMBERS * CAP

    def one_member(index):
        picks = jnp.nonzero(member_ids == index, size=limit, fill_value=COLUMNS)[0].astype(jnp.int32)
        result_rows = run_member(padded_cols[picks], w_in[index], bias_in[index], w_mid[index], bias_mid[index], w_out[index])
        return (picks, result_rows)
    picks_all, results = lax.map(one_member, jnp.arange(MEMBERS, dtype=jnp.int32))
    outputs = jnp.zeros((COLUMNS + 1, FEAT + NFLUX), jnp.bfloat16)
    outputs = outputs.at[picks_all.reshape(-1)].set(results.reshape(-1, FEAT + NFLUX))[:COLUMNS]
    new_cols = grid_cols + outputs[:, :FEAT].astype(jnp.float32)
    new_state = new_cols.reshape(N_GX, N_GY, local_x, local_y, FEAT).transpose(0, 2, 1, 3, 4).reshape(NXN, NYN, FEAT)
    fluxes = outputs[:, FEAT:]
    flux_blocks = fluxes.reshape(DEVICES, EL_X, 4, EL_Y, 4, NFLUX).transpose(0, 1, 3, 2, 4, 5).reshape(DEVICES * ABLK, 16, NFLUX)
    element_ids = jnp.arange(INTERSECTIONS, dtype=jnp.int32) // LIST_DEV * ABLK + intersection_element
    picked = flux_blocks[element_ids]
    regrid_blocks = regrid_weight.reshape(INTERSECTIONS, 16, OCELL)
    contribution = jnp.einsum('kcf,kco->kfo', picked.astype(jnp.float32), regrid_blocks, precision=HIGHEST).reshape(INTERSECTIONS, NFLUX * OCELL)
    target = ocean_owner[:, 0] * OB_DEV + ocean_block
    ocean_total = jax.ops.segment_sum(contribution, target, num_segments=NOB)
    return (new_state, ocean_total)
```

```python
import math

import jax
import jax.numpy as jnp
import numpy as np
from jax import lax
from jax.sharding import PartitionSpec as P

LEV = 64
OB_DEV = 16


STEP_DT = 0.2
HIGHEST = lax.Precision.HIGHEST


def padded_2(value, sides, width):
    for axis, dim in sides:
        count, length = (lax.axis_size(axis), value.shape[dim])
        up = [(i, (i + 1) % count) for i in range(count)]
        down = [(j, i) for i, j in up]
        last = lax.slice_in_dim(value, length - width, length, axis=dim)
        leading = lax.slice_in_dim(value, 0, width, axis=dim)
        before = lax.ppermute(last, axis, up)
        after = lax.ppermute(leading, axis, down)
        value = jnp.concatenate([before, value, after], axis=dim)
    return value


def derivative_table():
    root = 1.0 / math.sqrt(5.0)
    nodes = np.array([-1.0, -root, root, 1.0])
    table = np.zeros((4, 4))
    for row_index in range(4):
        for col_index in range(4):
            if row_index == col_index:
                table[row_index, col_index] = sum(
                    (
                        1.0 / (nodes[row_index] - nodes[other])
                        for other in range(4)
                        if other != row_index
                    )
                )
            else:
                weight_row = np.prod(
                    [nodes[row_index] - nodes[other] for other in range(4) if other != row_index]
                )
                weight_col = np.prod(
                    [nodes[col_index] - nodes[other] for other in range(4) if other != col_index]
                )
                table[row_index, col_index] = weight_row / (
                    weight_col * (nodes[row_index] - nodes[col_index])
                )
    return table


def element_tendency(field, deriv_table, levels):
    size_x, size_y, features = field.shape
    along_x = jnp.einsum(
        "ij,ejyf->eiyf",
        deriv_table,
        field.reshape(size_x // 4, 4, size_y, features),
        precision=HIGHEST,
    )
    along_y = jnp.einsum(
        "ij,xejf->xeif",
        deriv_table,
        field.reshape(size_x, size_y // 4, 4, features),
        precision=HIGHEST,
    )
    grid = field.reshape(size_x, size_y, 4, levels)
    wind_u = grid[:, :, 2:3, :]
    wind_v = grid[:, :, 3:4, :]
    tendency = -(
        wind_u * along_x.reshape(size_x, size_y, 4, levels)
        + wind_v * along_y.reshape(size_x, size_y, 4, levels)
    )
    return tendency.reshape(size_x, size_y, features)


def slot_positions(owners, capacity, peer_count):
    one_hot = (owners[:, None] == jnp.arange(peer_count, dtype=jnp.int32)[None, :]).astype(
        jnp.int32
    )
    rank = jnp.sum(jnp.cumsum(one_hot, axis=0) * one_hot, axis=1) - 1
    return owners * capacity + rank


def run_member(flat_rows, weights):
    w_first, b_first, w_second, b_second, w_last = weights
    hidden_one = jax.nn.silu(
        jnp.dot(flat_rows, w_first, preferred_element_type=jnp.float32) + b_first
    ).astype(jnp.bfloat16)
    hidden_two = jax.nn.silu(
        jnp.dot(hidden_one, w_second, preferred_element_type=jnp.float32) + b_second
    ).astype(jnp.bfloat16)
    return jnp.dot(hidden_two, w_last, preferred_element_type=jnp.float32).astype(jnp.bfloat16)


def shards(
    state,
    group_member,
    w_in,
    bias_in,
    w_mid,
    bias_mid,
    w_out,
    intersection_element,
    ocean_owner,
    ocean_block,
    regrid_weight,
):
    size_x, size_y, features = state.shape
    deriv_table = jnp.asarray(derivative_table(), dtype=jnp.float32)
    tendency = element_tendency(state, deriv_table, LEV)
    padded = padded_2(tendency, (("gx", 0), ("gy", 1)), 1)
    row_phase = (jnp.arange(size_x) % 4)[:, None, None]
    middle = padded[1:-1]
    along_x = jnp.where(
        row_phase == 0,
        0.5 * (middle + padded[:-2]),
        jnp.where(row_phase == 3, 0.5 * (middle + padded[2:]), middle),
    )
    col_phase = (jnp.arange(size_y) % 4)[None, :, None]
    centre = along_x[:, 1:-1]
    smooth = jnp.where(
        col_phase == 0,
        0.5 * (centre + along_x[:, :-2]),
        jnp.where(col_phase == 3, 0.5 * (centre + along_x[:, 2:]), centre),
    )
    advanced = state + STEP_DT * smooth
    col_count = size_x * size_y
    columns = advanced.reshape(col_count, features).astype(jnp.bfloat16)
    grid_x = lax.axis_size("gx")
    grid_y = lax.axis_size("gy")
    devices = grid_x * grid_y
    capacity = 2 * col_count // devices
    slot_index = slot_positions(group_member[:, 0], capacity, devices)
    send_buffer = (
        jnp.zeros((devices * capacity, features), jnp.bfloat16).at[slot_index].set(columns)
    )
    weights = (w_in[0], bias_in[0], w_mid[0], bias_mid[0], w_out[0])
    received = lax.all_to_all(
        send_buffer.reshape(devices, capacity, features),
        ("gx", "gy"),
        split_axis=0,
        concat_axis=0,
        tiled=True,
    )
    lead_shape = received.shape[:-1]
    result_rows = run_member(received.reshape(-1, features), weights)
    answered = result_rows.reshape(lead_shape + (result_rows.shape[-1],))
    returned = lax.all_to_all(answered, ("gx", "gy"), split_axis=0, concat_axis=0, tiled=True)
    outputs = returned.reshape(devices * capacity, -1)[slot_index]
    new_state = advanced + outputs[:, :features].astype(jnp.float32).reshape(
        size_x, size_y, features
    )
    fluxes = outputs[:, features:]
    flux_count = fluxes.shape[1]
    flux_blocks = (
        fluxes.reshape(size_x // 4, 4, size_y // 4, 4, flux_count)
        .transpose(0, 2, 1, 3, 4)
        .reshape(-1, 16, flux_count)
    )
    picked = flux_blocks[intersection_element]
    intersection_count = picked.shape[0]
    regrid_blocks = regrid_weight.reshape(intersection_count, 16, -1)
    contribution = jnp.einsum(
        "kcf,kco->kfo", picked.astype(jnp.float32), regrid_blocks, precision=HIGHEST
    ).reshape(intersection_count, -1)
    owners = ocean_owner[:, 0]
    ocean_capacity = 2 * intersection_count // devices
    ocean_slot = slot_positions(owners, ocean_capacity, devices)
    ocean_rows = devices * ocean_capacity
    width = contribution.shape[1]
    ocean_send = jnp.zeros((ocean_rows, width), jnp.float32).at[ocean_slot].set(contribution)
    block_send = jnp.zeros((ocean_rows,), jnp.int32).at[ocean_slot].set(ocean_block)
    block_got = lax.all_to_all(
        block_send.reshape(devices, ocean_capacity),
        ("gx", "gy"),
        split_axis=0,
        concat_axis=0,
        tiled=True,
    ).reshape(-1)
    ocean_got = lax.all_to_all(
        ocean_send.reshape(devices, ocean_capacity, width),
        ("gx", "gy"),
        split_axis=0,
        concat_axis=0,
        tiled=True,
    ).reshape(ocean_rows, width)
    pick = (block_got[None, :] == jnp.arange(OB_DEV, dtype=jnp.int32)[:, None]).astype(jnp.float32)
    ocean_total = jnp.dot(pick, ocean_got, precision=HIGHEST)
    return (new_state, ocean_total)


def solution(mesh):
    return jax.shard_map(
        shards,
        mesh=mesh,
        in_specs=(
            P("gx", "gy", None),
            P(("gx", "gy"), None),
            P(("gx", "gy"), None, None),
            P(("gx", "gy"), None),
            P(("gx", "gy"), None, None),
            P(("gx", "gy"), None),
            P(("gx", "gy"), None, None),
            P(("gx", "gy")),
            P(("gx", "gy"), None),
            P(("gx", "gy")),
            P(("gx", "gy"), None),
        ),
        out_specs=(P("gx", "gy", None), P(("gx", "gy"), None)),
        check_vma=False,
    )
```

```python
import math

import jax
import jax.numpy as jnp
import numpy as np
from jax import lax
from jax.experimental import pallas as pl
from jax.experimental.pallas import tpu as pltpu
from jax.sharding import PartitionSpec as P

LEV = 64
OB_DEV = 16
STEP_DT = 0.2
HIGHEST = lax.Precision.HIGHEST
AXES = ("gx", "gy")
F32 = jnp.float32
BF16 = jnp.bfloat16
MIB = 1 << 20


def derivative_table():
    root = 1.0 / math.sqrt(5.0)
    nodes = np.array([-1.0, -root, root, 1.0])
    table = np.zeros((4, 4))
    for row_index in range(4):
        for col_index in range(4):
            if row_index == col_index:
                table[row_index, col_index] = sum(
                    (
                        1.0 / (nodes[row_index] - nodes[other])
                        for other in range(4)
                        if other != row_index
                    )
                )
            else:
                weight_row = np.prod(
                    [nodes[row_index] - nodes[other] for other in range(4) if other != row_index]
                )
                weight_col = np.prod(
                    [nodes[col_index] - nodes[other] for other in range(4) if other != col_index]
                )
                table[row_index, col_index] = weight_row / (
                    weight_col * (nodes[row_index] - nodes[col_index])
                )
    return table


TABLE = [[float(np.float32(v)) for v in row] for row in derivative_table()]


def iota(shape, dim):
    return lax.broadcasted_iota(jnp.int32, shape, dim)


def dot(a, b, precision=None):
    return jnp.dot(a, b, preferred_element_type=F32, precision=precision)


def along_rows(line):
    rows, features = line.shape
    groups = line.reshape(rows // 8, 8, features)
    phase = iota((1, 8, features), 1) % 4
    total = None
    for offset in range(-3, 4):
        weight = jnp.zeros((1, 8, features), F32)
        for p in range(4):
            if 0 <= p + offset < 4:
                weight = jnp.where(phase == p, TABLE[p][p + offset], weight)
        moved = groups if offset == 0 else pltpu.roll(groups, (-offset) % 8, 1)
        total = weight * moved if total is None else total + weight * moved
    return total.reshape(rows, features)


def winds(line):
    pair = line[:, 128:]
    swapped = pltpu.roll(pair, LEV, 1)
    first = iota(pair.shape, 1) < LEV
    return jnp.where(first, pair, swapped), jnp.where(first, swapped, pair)


def advect(line, along_x, along_y):
    u, v = winds(line)
    return jnp.concatenate(
        [
            -(u * along_x[:, :128] + v * along_y[:, :128]),
            -(u * along_x[:, 128:] + v * along_y[:, 128:]),
        ],
        axis=1,
    )


def across(lines, i):
    total = TABLE[i][0] * lines[0]
    for j in range(1, 4):
        total = total + TABLE[i][j] * lines[j]
    return total


def smooth_rows(line):
    rows, features = line.shape
    row = iota((rows, features), 0)
    phase = row % 4
    before = jnp.where(row == 0, 0.0, pltpu.roll(line, 1, 0))
    after = jnp.where(row == rows - 1, 0.0, pltpu.roll(line, rows - 1, 0))
    return jnp.where(
        phase == 0,
        0.5 * (line + before),
        jnp.where(phase == 3, 0.5 * (line + after), line),
    )


def edges_kernel(state, x_low, x_high, y_low, y_high):
    size_x, size_y, _ = state.shape
    for out, base, i in ((x_low, 0, 0), (x_high, size_x - 4, 3)):
        lines = [state[base + j] for j in range(4)]
        out[...] = advect(lines[i], across(lines, i), along_rows(lines[i]))
    for out, base, i in ((y_low, 0, 0), (y_high, size_y - 4, 3)):
        lines = [state[:, base + j, :] for j in range(4)]
        out[...] = advect(lines[i], along_rows(lines[i]), across(lines, i))


def sides_kernel(y_low, y_high, x_before, x_after, partial, low, high):
    size, features = y_low.shape
    row = iota((size, features), 0)
    for out, line, y in ((low, y_low, 0), (high, y_high, size - 1)):
        extra = jnp.where(
            row == 0,
            0.5 * x_before[y : y + 1, :],
            jnp.where(row == size - 1, 0.5 * x_after[y : y + 1, :], 0.0),
        )
        out[...] = smooth_rows(line[...]) + extra


def local_kernel(state, token, partial, tend):
    size_x, size_y, features = state.shape
    tend[0] = jnp.zeros((size_y, features), F32)
    tend[size_x + 1] = jnp.zeros((size_y, features), F32)

    @pl.loop(0, size_x // 4)
    def _(e):
        lines = [state[4 * e + j] for j in range(4)]
        for i in range(4):
            tend[4 * e + i + 1] = advect(lines[i], across(lines, i), along_rows(lines[i]))

    @pl.loop(0, size_x // 4)
    def _(e):
        low = 4 * e + 1
        values = [
            0.5 * (tend[low] + tend[low - 1]),
            tend[low + 1],
            tend[low + 2],
            0.5 * (tend[low + 3] + tend[low + 4]),
        ]
        for i in range(4):
            partial[4 * e + i] = state[4 * e + i] + STEP_DT * smooth_rows(values[i])


def owner_ranks(owners):
    count = owners.shape[1]
    earlier = (iota((count, count), 0) < iota((count, count), 1)).astype(F32).astype(BF16)
    hot = (iota((128, count), 0) == owners).astype(F32)
    rank = jnp.sum(dot(hot.astype(BF16), earlier) * hot, axis=0, keepdims=True)
    return hot, rank.astype(jnp.int32)


def route_kernel(capacity, member_row, slot_row, hot_rows):
    columns = member_row.shape[1]
    earlier = (iota((128, 128), 0) < iota((128, 128), 1)).astype(F32).astype(BF16)
    seen = jnp.zeros((128, 1), F32)
    for b in range(columns // 128):
        part = slice(b * 128, (b + 1) * 128)
        members = member_row[:, part]
        hot = (iota((128, 128), 0) == members).astype(F32)
        count = dot(hot.astype(BF16), earlier) + seen
        rank = jnp.sum(count * hot, axis=0, keepdims=True).astype(jnp.int32)
        slots = members * capacity + rank
        slot_row[:, part] = slots
        seen = seen + jnp.sum(hot, axis=1, keepdims=True)
    step = 256
    slots = slot_row[...]
    for b in range(hot_rows.shape[0] // step):
        hot = iota((step, columns), 0) + b * step == slots
        hot_rows[b * step : (b + 1) * step, :] = hot.astype(F32).astype(BF16)


def add_outside(advanced, partial, x_before, x_after, y_before, y_after):
    size_x, size_y, _ = partial.shape
    advanced[...] = partial[...]
    half = 0.5 * STEP_DT
    advanced[0] = advanced[0] + half * smooth_rows(x_before[...])
    advanced[size_x - 1] = advanced[size_x - 1] + half * smooth_rows(x_after[...])
    advanced[:, 0, :] = advanced[:, 0, :] + half * y_before[...]
    advanced[:, size_y - 1, :] = advanced[:, size_y - 1, :] + half * y_after[...]


def pack_kernel(
    partial, x_before, x_after, y_before, y_after, hot_rows, send_out, advanced, send, sems
):
    size_x, size_y, features = partial.shape
    add_outside(advanced, partial, x_before, x_after, y_before, y_after)
    columns = advanced[...].reshape(size_x * size_y, features).astype(BF16)
    step = 256
    copies = []
    for b in range(send.shape[0] // step):
        part = slice(b * step, (b + 1) * step)
        send[part, :] = dot(hot_rows[part, :], columns).astype(BF16)
        copy = pltpu.make_async_copy(send.at[part], send_out.at[part], sems.at[b])
        copy.start()
        copies.append(copy)
    for copy in copies:
        copy.wait()


def as_column(row):
    wide = jnp.where(iota((128, 128), 0) == iota((128, 128), 1), row, 0)
    return jnp.sum(wide, axis=1, keepdims=True)


def prepare_kernel(capacity, element_row, weight, slot_row, token, places, tiled):
    count = element_row.shape[1]
    lane = iota((count, 128), 1)
    for c in range(16):
        part = weight[:, (c // 8) * 128 : (c // 8 + 1) * 128]
        part = jnp.where(lane // 16 == c % 8, part, 0.0)
        for distance in (64, 32, 16):
            part = part + pltpu.roll(part, distance, 1)
        tiled[c] = part

    columns = slot_row.shape[1]
    lane = iota((128, 128), 1)
    table = []
    for b in range(columns // 128):
        slots = as_column(slot_row[:, b * 128 : (b + 1) * 128])
        both = jnp.where(lane == 0, slots // capacity, jnp.where(lane == 1, slots % capacity, 0))
        table.append(both.astype(F32).astype(BF16))
    table = jnp.concatenate(table, axis=0)
    element = as_column(element_row[...])
    base = (element // 8) * 128 + (element % 8) * 4
    place = iota((count, columns), 1)
    slots = jnp.zeros((count, 128), F32)
    for c in range(16):
        hot = (place == base + (c // 4) * 32 + c % 4).astype(F32).astype(BF16)
        both = dot(hot, table)
        slots = jnp.where(lane == c, both[:, 0:1] * capacity + both[:, 1:2], slots)
    places[...] = slots.astype(jnp.int32)


def silu(x):
    half = 0.5 * x
    return half + half * jnp.tanh(half)


def first_kernel(rows, w_in, b_in, owner_row, block_row, out, blocks):
    owners = owner_row[...]
    hot, rank = owner_ranks(owners)
    values = block_row[...].astype(F32)
    lane = iota(blocks.shape, 1)
    first = jnp.sum(jnp.where(rank == 0, hot, 0.0) * values, axis=1, keepdims=True)
    second = jnp.sum(jnp.where(rank == 1, hot, 0.0) * values, axis=1, keepdims=True)
    blocks[...] = jnp.where(lane == 0, first, jnp.where(lane == 1, second, 0.0))

    step = 512
    for b in range(rows.shape[0] // step):
        part = slice(b * step, (b + 1) * step)
        out[part, :] = silu(dot(rows[part, :], w_in[0]) + b_in[...]).astype(BF16)


def second_kernel(first, w_mid, b_mid, w_out, w_flux, blocks, answer, token):
    step = 512
    sources = step // 16
    lane = iota((step, 128), 1)
    own = lane // 8 == iota((step, 128), 0) % 16
    line = iota((sources, 8, 128), 1)
    for b in range(first.shape[0] // step):
        hidden = dot(first[b * step : (b + 1) * step, :], w_mid[0])
        hidden = silu(hidden + b_mid[...]).astype(BF16)
        tends = dot(hidden, w_out[0, :, 0:256]).astype(BF16)
        part = slice(b * sources, (b + 1) * sources)
        answer[part, 0:16, :] = tends[:, :128].reshape(sources, 16, 128)
        answer[part, 16:32, :] = tends[:, 128:].reshape(sources, 16, 128)
        flux = jnp.where(own, dot(hidden, w_flux[...]), 0.0)
        flux = jnp.sum(flux.reshape(sources, 16, 128), axis=1, keepdims=True)
        names = blocks[part, :].reshape(sources, 1, 128)
        tail = jnp.where(line == 0, flux, jnp.where(line == 1, names, 0.0))
        answer[part, 32:40, :] = tail.astype(BF16)
    token[...] = blocks[0:8, :]


def contribution_kernel(capacity, answer, places, tiled, owner_row, send):
    flux = answer[:, 32:40, :].astype(F32)[:, 0, :].astype(BF16)
    spread = (iota((128, 128), 0) % 8 == iota((128, 128), 1) // 16).astype(F32).astype(BF16)
    lane = iota((128, 128), 1)
    total = None
    for c in range(16):
        slots = places[:, c : c + 1]
        pick = (lane == slots // capacity).astype(F32).astype(BF16)
        value = jnp.where(lane // 8 == slots % capacity, dot(pick, flux), 0.0)
        term = dot(value.astype(BF16), spread) * tiled[c]
        total = term if total is None else total + term
    owners = owner_row[...]
    _, rank = owner_ranks(owners)
    hot = (iota(send.shape, 0) == owners * 2 + rank).astype(F32)
    send[...] = dot(hot, total, HIGHEST)


def columns_kernel(
    answer,
    slot_row,
    partial,
    x_before,
    x_after,
    y_before,
    y_after,
    new_state,
    sums,
    rows,
    advanced,
):
    sources = answer.shape[0]
    slots = sources * 16
    size_x, size_y, features = partial.shape
    add_outside(advanced, partial, x_before, x_after, y_before, y_after)
    rows[:, 0:128] = answer[:, 0:16, :].reshape(slots, 128)
    rows[:, 128:256] = answer[:, 16:32, :].reshape(slots, 128)
    step = 128
    lines = step // size_y
    for b in range(size_x // lines):
        hot = iota((step, slots), 1) == as_column(slot_row[:, b * step : (b + 1) * step])
        tends = dot(hot.astype(F32).astype(BF16), rows[...])
        part = slice(b * lines, (b + 1) * lines)
        new_state[part] = advanced[part] + tends.reshape(lines, size_y, features)
    names = answer[:, 32:40, :].astype(F32)[:, 1, :]
    lane = iota((sources, 128), 1)
    for j in range(2):
        hot = (names[:, j : j + 1].astype(jnp.int32) == lane).astype(F32)
        sums[j] = jnp.transpose(hot)[:OB_DEV, :]


def ocean_kernel(received, sums, out):
    out[...] = dot(sums[0], received[:, 0, :], HIGHEST) + dot(sums[1], received[:, 1, :], HIGHEST)


def call(kernel, outs, *args, flops=0, nbytes=0, transcendentals=0, scratch=(), limit=16, spaces=None, out_spaces=None):
    return pl.pallas_call(
        kernel,
        out_shape=[jax.ShapeDtypeStruct(s, d) for s, d in outs],
        in_specs=[
            pl.BlockSpec(memory_space=(spaces or {}).get(i, pltpu.VMEM)) for i in range(len(args))
        ],
        out_specs=[
            pl.BlockSpec(memory_space=(out_spaces or {}).get(i, pltpu.VMEM))
            for i in range(len(outs))
        ],
        scratch_shapes=list(scratch),
        compiler_params=pltpu.CompilerParams(vmem_limit_bytes=limit * MIB),
        cost_estimate=pl.CostEstimate(
            flops=flops, bytes_accessed=nbytes, transcendentals=transcendentals
        ),
    )(*args)


def shift(value, axis, step):
    size = lax.axis_size(axis)
    return lax.ppermute(value, axis, [(i, (i + step) % size) for i in range(size)])


def exchange(value):
    return lax.all_to_all(value, AXES, split_axis=0, concat_axis=0, tiled=True)


def shards(
    state,
    group_member,
    w_in,
    bias_in,
    w_mid,
    bias_mid,
    w_out,
    intersection_element,
    ocean_owner,
    ocean_block,
    regrid_weight,
):
    size_x, size_y, features = state.shape
    devices = lax.axis_size("gx") * lax.axis_size("gy")
    columns = size_x * size_y
    capacity = 2 * columns // devices
    slots = devices * capacity
    count = intersection_element.shape[0]
    line = ((size_x, features), F32)

    x_low, x_high, y_low, y_high = call(
        edges_kernel,
        [line] * 4,
        state,
        nbytes=2 * MIB,
        flops=MIB,
    )
    x_before, x_after = shift(x_high, "gx", 1), shift(x_low, "gx", -1)

    def local(token):
        return call(
            local_kernel,
            [(state.shape, F32)],
            state,
            token,
            nbytes=8 * MIB,
            flops=64 * MIB,
            spaces={1: pl.ANY},
            scratch=[pltpu.VMEM((size_x + 2, size_y, features), F32)],
        )[0]

    partial = local(x_low)
    low, high = call(
        sides_kernel,
        [line] * 2,
        y_low,
        y_high,
        x_before,
        x_after,
        partial,
        spaces={4: pl.ANY},
    )
    y_before, y_after = shift(high, "gy", 1), shift(low, "gy", -1)
    slot_row, hot_rows = call(
        lambda *refs: route_kernel(capacity, *refs),
        [((1, columns), jnp.int32), ((slots, columns), BF16)],
        group_member.reshape(1, columns),
        nbytes=8 * MIB,
        flops=64 * MIB,
    )
    (send,) = call(
        pack_kernel,
        [((slots, features), BF16)],
        partial,
        x_before,
        x_after,
        y_before,
        y_after,
        hot_rows,
        nbytes=4 * MIB,
        flops=2 * slots * columns * features,
        out_spaces={0: pl.ANY},
        scratch=[
            pltpu.VMEM(state.shape, F32),
            pltpu.VMEM((slots, features), BF16),
            pltpu.SemaphoreType.DMA((8,)),
        ],
    )
    received = exchange(send.reshape(devices, capacity, features)).reshape(slots, features)

    w_flux = jnp.tile(w_out[0, :, features:], (1, 16))
    hidden = w_in.shape[2]
    owner_row = ocean_owner.reshape(1, count)
    first, blocks = call(
        first_kernel,
        [((slots, hidden), BF16), ((devices, 128), F32)],
        received,
        w_in,
        bias_in,
        owner_row,
        ocean_block.reshape(1, count),
        nbytes=6 * MIB,
        flops=2 * slots * features * hidden,
        transcendentals=slots * hidden,
    )
    answered, token = call(
        second_kernel,
        [((devices, 40, 128), BF16), ((8, 128), F32)],
        first,
        w_mid,
        bias_mid,
        w_out,
        w_flux,
        blocks,
        nbytes=8 * MIB,
        flops=2 * slots * hidden * (hidden + 384),
        transcendentals=slots * hidden,
        limit=20,
    )
    answer = exchange(answered)
    places, tiled = call(
        lambda *refs: prepare_kernel(capacity, *refs),
        [((count, 128), jnp.int32), ((16, count, 128), F32)],
        intersection_element.reshape(1, count),
        regrid_weight,
        slot_row,
        token,
        nbytes=12 * MIB,
        flops=2 * 16 * count * columns * 256,
    )
    (ocean_send,) = call(
        lambda *refs: contribution_kernel(capacity, *refs),
        [((2 * devices, 128), F32)],
        answer,
        places,
        tiled,
        owner_row,
        nbytes=4 * MIB,
        flops=2 * 2 * 2048 * 128 * 128,
    )
    ocean_got = exchange(ocean_send.reshape(devices, 2, 128))
    partial = local(ocean_send)
    new_state, sums = call(
        columns_kernel,
        [(state.shape, F32), ((2, OB_DEV, devices), F32)],
        answer,
        slot_row,
        partial,
        x_before,
        x_after,
        y_before,
        y_after,
        nbytes=12 * MIB,
        flops=2 * slots * columns * features,
        scratch=[pltpu.VMEM((slots, features), BF16), pltpu.VMEM(state.shape, F32)],
    )
    (ocean_total,) = call(
        ocean_kernel, [((OB_DEV, 128), F32)], ocean_got, sums, nbytes=MIB, flops=MIB
    )
    return (new_state, ocean_total)


def solution(mesh):
    return jax.shard_map(
        shards,
        mesh=mesh,
        in_specs=(
            P("gx", "gy", None),
            P(("gx", "gy"), None),
            P(("gx", "gy"), None, None),
            P(("gx", "gy"), None),
            P(("gx", "gy"), None, None),
            P(("gx", "gy"), None),
            P(("gx", "gy"), None, None),
            P(("gx", "gy")),
            P(("gx", "gy"), None),
            P(("gx", "gy")),
            P(("gx", "gy"), None),
        ),
        out_specs=(P("gx", "gy", None), P(("gx", "gy"), None)),
        check_vma=False,
    )
```

```python
import math

import jax
import jax.numpy as jnp
import numpy as np
from jax import lax
from jax.experimental import pallas as pl
from jax.experimental.pallas import tpu as pltpu
from jax.sharding import PartitionSpec as P

LEV = 64
OB_DEV = 16
STEP_DT = 0.2
HIGHEST = lax.Precision.HIGHEST
AXES = ("gx", "gy")
F32 = jnp.float32
BF16 = jnp.bfloat16
MIB = 1 << 20


def derivative_table():
    root = 1.0 / math.sqrt(5.0)
    nodes = np.array([-1.0, -root, root, 1.0])
    table = np.zeros((4, 4))
    for row_index in range(4):
        for col_index in range(4):
            if row_index == col_index:
                table[row_index, col_index] = sum(
                    (
                        1.0 / (nodes[row_index] - nodes[other])
                        for other in range(4)
                        if other != row_index
                    )
                )
            else:
                weight_row = np.prod(
                    [nodes[row_index] - nodes[other] for other in range(4) if other != row_index]
                )
                weight_col = np.prod(
                    [nodes[col_index] - nodes[other] for other in range(4) if other != col_index]
                )
                table[row_index, col_index] = weight_row / (
                    weight_col * (nodes[row_index] - nodes[col_index])
                )
    return table


TABLE = [[float(np.float32(v)) for v in row] for row in derivative_table()]


def iota(shape, dim):
    return lax.broadcasted_iota(jnp.int32, shape, dim)


def dot(a, b, precision=None):
    return jnp.dot(a, b, preferred_element_type=F32, precision=precision)


def along_rows(line):
    rows, features = line.shape
    groups = line.reshape(rows // 8, 8, features)
    phase = iota((1, 8, features), 1) % 4
    total = None
    for offset in range(-3, 4):
        weight = jnp.zeros((1, 8, features), F32)
        for p in range(4):
            if 0 <= p + offset < 4:
                weight = jnp.where(phase == p, TABLE[p][p + offset], weight)
        moved = groups if offset == 0 else pltpu.roll(groups, (-offset) % 8, 1)
        total = weight * moved if total is None else total + weight * moved
    return total.reshape(rows, features)


def winds(line):
    pair = line[:, 128:]
    swapped = pltpu.roll(pair, LEV, 1)
    first = iota(pair.shape, 1) < LEV
    return jnp.where(first, pair, swapped), jnp.where(first, swapped, pair)


def advect(line, along_x, along_y):
    u, v = winds(line)
    return jnp.concatenate(
        [
            -(u * along_x[:, :128] + v * along_y[:, :128]),
            -(u * along_x[:, 128:] + v * along_y[:, 128:]),
        ],
        axis=1,
    )


def across(lines, i):
    total = TABLE[i][0] * lines[0]
    for j in range(1, 4):
        total = total + TABLE[i][j] * lines[j]
    return total


def smooth_rows(line):
    rows, features = line.shape
    row = iota((rows, features), 0)
    phase = row % 4
    before = jnp.where(row == 0, 0.0, pltpu.roll(line, 1, 0))
    after = jnp.where(row == rows - 1, 0.0, pltpu.roll(line, rows - 1, 0))
    return jnp.where(
        phase == 0,
        0.5 * (line + before),
        jnp.where(phase == 3, 0.5 * (line + after), line),
    )


def edges_kernel(state, x_low, x_high, y_low, y_high):
    size_x, size_y, _ = state.shape
    for out, base, i in ((x_low, 0, 0), (x_high, size_x - 4, 3)):
        lines = [state[base + j] for j in range(4)]
        out[...] = advect(lines[i], across(lines, i), along_rows(lines[i]))
    for out, base, i in ((y_low, 0, 0), (y_high, size_y - 4, 3)):
        lines = [state[:, base + j, :] for j in range(4)]
        out[...] = advect(lines[i], along_rows(lines[i]), across(lines, i))


def sides_kernel(y_low, y_high, x_before, x_after, partial, slot_row, low, high):
    size, features = y_low.shape
    row = iota((size, features), 0)
    for out, line, y in ((low, y_low, 0), (high, y_high, size - 1)):
        extra = jnp.where(
            row == 0,
            0.5 * x_before[y : y + 1, :],
            jnp.where(row == size - 1, 0.5 * x_after[y : y + 1, :], 0.0),
        )
        out[...] = smooth_rows(line[...]) + extra


def local_kernel(state, token, partial, tend):
    size_x, size_y, features = state.shape
    tend[0] = jnp.zeros((size_y, features), F32)
    tend[size_x + 1] = jnp.zeros((size_y, features), F32)

    @pl.loop(0, size_x // 4)
    def _(e):
        lines = [state[4 * e + j] for j in range(4)]
        for i in range(4):
            tend[4 * e + i + 1] = advect(lines[i], across(lines, i), along_rows(lines[i]))

    @pl.loop(0, size_x // 4)
    def _(e):
        low = 4 * e + 1
        values = [
            0.5 * (tend[low] + tend[low - 1]),
            tend[low + 1],
            tend[low + 2],
            0.5 * (tend[low + 3] + tend[low + 4]),
        ]
        for i in range(4):
            partial[4 * e + i] = state[4 * e + i] + STEP_DT * smooth_rows(values[i])


def owner_ranks(owners):
    count = owners.shape[1]
    earlier = (iota((count, count), 0) < iota((count, count), 1)).astype(F32).astype(BF16)
    hot = (iota((128, count), 0) == owners).astype(F32)
    rank = jnp.sum(dot(hot.astype(BF16), earlier) * hot, axis=0, keepdims=True)
    return hot, rank.astype(jnp.int32)


def route_kernel(capacity, size_y, member_row, slot_row, hot_rows, hot_sides):
    columns = member_row.shape[1]
    size_x = columns // size_y
    earlier = (iota((128, 128), 0) < iota((128, 128), 1)).astype(F32).astype(BF16)
    seen = jnp.zeros((128, 1), F32)
    for b in range(columns // 128):
        part = slice(b * 128, (b + 1) * 128)
        members = member_row[:, part]
        hot = (iota((128, 128), 0) == members).astype(F32)
        count = dot(hot.astype(BF16), earlier) + seen
        rank = jnp.sum(count * hot, axis=0, keepdims=True).astype(jnp.int32)
        slot_row[:, part] = members * capacity + rank
        seen = seen + jnp.sum(hot, axis=1, keepdims=True)
    step = 256
    slots = slot_row[...]
    for b in range(hot_rows.shape[0] // step):
        hot = iota((step, columns), 0) + b * step == slots
        hot_rows[b * step : (b + 1) * step, :] = hot.astype(F32).astype(BF16)
    lane = iota((columns, 128), 1)
    place = (lane % size_x) * size_y + (lane // size_x) * (size_y - 1)
    choose = ((iota((columns, 128), 0) == place) & (lane < 2 * size_x)).astype(F32).astype(BF16)
    row = iota((8, columns), 0)
    both = jnp.where(row == 0, slots // capacity, jnp.where(row == 1, slots % capacity, 0))
    both = dot(both.astype(F32).astype(BF16), choose).astype(jnp.int32)
    side = both[0:1, :] * capacity + both[1:2, :]
    side = jnp.where(iota((1, 128), 1) < 2 * size_x, side, -1)
    for b in range(hot_sides.shape[0] // step):
        hot = iota((step, 128), 0) + b * step == side
        hot_sides[b * step : (b + 1) * step, :] = hot.astype(F32).astype(BF16)


def add_before_after(advanced, partial, x_before, x_after):
    size_x, _, _ = partial.shape
    advanced[...] = partial[...]
    half = 0.5 * STEP_DT
    advanced[0] = advanced[0] + half * smooth_rows(x_before[...])
    advanced[size_x - 1] = advanced[size_x - 1] + half * smooth_rows(x_after[...])


def inner_kernel(partial, x_before, x_after, hot_rows, send, sides, advanced):
    size_x, size_y, features = partial.shape
    add_before_after(advanced, partial, x_before, x_after)
    for i, y in enumerate((0, size_y - 1)):
        sides[i * size_x : (i + 1) * size_x, :] = advanced[:, y, :]
        advanced[:, y, :] = jnp.zeros((size_x, features), F32)
    columns = advanced[...].reshape(size_x * size_y, features).astype(BF16)
    step = 256
    for b in range(send.shape[0] // step):
        part = slice(b * step, (b + 1) * step)
        send[part, :] = dot(hot_rows[part, :], columns).astype(BF16)


def pack_kernel(inner, sides, y_before, y_after, hot_sides, send_out, send, sems):
    half = 0.5 * STEP_DT
    size, features = y_before.shape
    columns = jnp.concatenate(
        [
            sides[0:size, :] + half * y_before[...],
            sides[size : 2 * size, :] + half * y_after[...],
            jnp.zeros((128 - 2 * size, features), F32),
        ],
        axis=0,
    ).astype(BF16)
    step = send.shape[0] // sems.shape[0]
    copies = []
    for b in range(sems.shape[0]):
        part = slice(b * step, (b + 1) * step)
        send[part, :] = inner[part, :] + dot(hot_sides[part, :], columns).astype(BF16)
        copy = pltpu.make_async_copy(send.at[part], send_out.at[part], sems.at[b])
        copy.start()
        copies.append(copy)
    for copy in copies:
        copy.wait()


def as_column(row):
    wide = jnp.where(iota((128, 128), 0) == iota((128, 128), 1), row, 0)
    return jnp.sum(wide, axis=1, keepdims=True)


def prepare_kernel(capacity, element_row, weight, slot_row, token, places, tiled):
    count = element_row.shape[1]
    lane = iota((count, 128), 1)
    for c in range(16):
        part = weight[:, (c // 8) * 128 : (c // 8 + 1) * 128]
        part = jnp.where(lane // 16 == c % 8, part, 0.0)
        for distance in (64, 32, 16):
            part = part + pltpu.roll(part, distance, 1)
        tiled[c] = part

    columns = slot_row.shape[1]
    lane = iota((128, 128), 1)
    table = []
    for b in range(columns // 128):
        slots = as_column(slot_row[:, b * 128 : (b + 1) * 128])
        both = jnp.where(lane == 0, slots // capacity, jnp.where(lane == 1, slots % capacity, 0))
        table.append(both.astype(F32).astype(BF16))
    table = jnp.concatenate(table, axis=0)
    element = as_column(element_row[...])
    base = (element // 8) * 128 + (element % 8) * 4
    place = iota((count, columns), 1)
    slots = jnp.zeros((count, 128), F32)
    for c in range(16):
        hot = (place == base + (c // 4) * 32 + c % 4).astype(F32).astype(BF16)
        both = dot(hot, table)
        slots = jnp.where(lane == c, both[:, 0:1] * capacity + both[:, 1:2], slots)
    places[...] = slots.astype(jnp.int32)


def silu_of_half(half):
    return half + half * jnp.tanh(half)


def first_kernel(rows, w_in, b_in, owner_row, block_row, out, blocks, w_half):
    owners = owner_row[...]
    hot, rank = owner_ranks(owners)
    values = block_row[...].astype(F32)
    lane = iota(blocks.shape, 1)
    first = jnp.sum(jnp.where(rank == 0, hot, 0.0) * values, axis=1, keepdims=True)
    second = jnp.sum(jnp.where(rank == 1, hot, 0.0) * values, axis=1, keepdims=True)
    blocks[...] = jnp.where(lane == 0, first, jnp.where(lane == 1, second, 0.0))

    w_half[...] = w_in[0] * jnp.asarray(0.5, BF16)
    b_half = 0.5 * b_in[...]
    step = 512
    for b in range(rows.shape[0] // step):
        part = slice(b * step, (b + 1) * step)
        out[part, :] = silu_of_half(dot(rows[part, :], w_half[...]) + b_half).astype(BF16)


def second_kernel(first, w_mid, b_mid, w_out, w_flux, blocks, answer, token, w_half, out, sems):
    step = first.shape[0] // sems.shape[0]
    sources = step // 16
    lane = iota((step, 128), 1)
    own = lane // 8 == iota((step, 128), 0) % 16
    line = iota((sources, 8, 128), 1)
    w_half[...] = w_mid[0] * jnp.asarray(0.5, BF16)
    b_half = 0.5 * b_mid[...]
    copies = []
    for b in range(sems.shape[0]):
        hidden = dot(first[b * step : (b + 1) * step, :], w_half[...])
        hidden = silu_of_half(hidden + b_half).astype(BF16)
        tends = dot(hidden, w_out[0, :, 0:256]).astype(BF16)
        part = slice(b * sources, (b + 1) * sources)
        out[part, 0:16, :] = tends[:, :128].reshape(sources, 16, 128)
        out[part, 16:32, :] = tends[:, 128:].reshape(sources, 16, 128)
        flux = jnp.where(own, dot(hidden, w_flux[...]), 0.0)
        flux = jnp.sum(flux.reshape(sources, 16, 128), axis=1, keepdims=True)
        names = blocks[part, :].reshape(sources, 1, 128)
        tail = jnp.where(line == 0, flux, jnp.where(line == 1, names, 0.0))
        out[part, 32:40, :] = tail.astype(BF16)
        copy = pltpu.make_async_copy(out.at[part], answer.at[part], sems.at[b])
        copy.start()
        copies.append(copy)
    token[...] = blocks[0:8, :]
    for copy in copies:
        copy.wait()


def contribution_kernel(capacity, answer, places, tiled, owner_row, send):
    flux = answer[:, 32:40, :].astype(F32)[:, 0, :].astype(BF16)
    spread = (iota((128, 128), 0) % 8 == iota((128, 128), 1) // 16).astype(F32).astype(BF16)
    lane = iota((128, 128), 1)
    total = None
    for c in range(16):
        slots = places[:, c : c + 1]
        pick = (lane == slots // capacity).astype(F32).astype(BF16)
        value = jnp.where(lane // 8 == slots % capacity, dot(pick, flux), 0.0)
        term = dot(value.astype(BF16), spread) * tiled[c]
        total = term if total is None else total + term
    owners = owner_row[...]
    _, rank = owner_ranks(owners)
    hot = (iota(send.shape, 0) == owners * 2 + rank).astype(F32)
    send[...] = dot(hot, total, HIGHEST)


def columns_kernel(
    answer,
    slot_row,
    partial,
    x_before,
    x_after,
    y_before,
    y_after,
    new_state,
    sums,
    rows,
    advanced,
):
    sources = answer.shape[0]
    slots = sources * 16
    size_x, size_y, features = partial.shape
    add_before_after(advanced, partial, x_before, x_after)
    half = 0.5 * STEP_DT
    advanced[:, 0, :] = advanced[:, 0, :] + half * y_before[...]
    advanced[:, size_y - 1, :] = advanced[:, size_y - 1, :] + half * y_after[...]
    rows[:, 0:128] = answer[:, 0:16, :].reshape(slots, 128)
    rows[:, 128:256] = answer[:, 16:32, :].reshape(slots, 128)
    step = 128
    lines = step // size_y
    for b in range(size_x // lines):
        hot = iota((step, slots), 1) == as_column(slot_row[:, b * step : (b + 1) * step])
        tends = dot(hot.astype(F32).astype(BF16), rows[...])
        part = slice(b * lines, (b + 1) * lines)
        new_state[part] = advanced[part] + tends.reshape(lines, size_y, features)
    names = answer[:, 32:40, :].astype(F32)[:, 1, :]
    lane = iota((sources, 128), 1)
    for j in range(2):
        hot = (names[:, j : j + 1].astype(jnp.int32) == lane).astype(F32)
        sums[j] = jnp.transpose(hot)[:OB_DEV, :]


def ocean_kernel(received, sums, out):
    out[...] = dot(sums[0], received[:, 0, :], HIGHEST) + dot(sums[1], received[:, 1, :], HIGHEST)


def call(kernel, outs, *args, flops=0, nbytes=0, transcendentals=0, scratch=(), limit=16, spaces=None, out_spaces=None):
    return pl.pallas_call(
        kernel,
        out_shape=[jax.ShapeDtypeStruct(s, d) for s, d in outs],
        in_specs=[
            pl.BlockSpec(memory_space=(spaces or {}).get(i, pltpu.VMEM)) for i in range(len(args))
        ],
        out_specs=[
            pl.BlockSpec(memory_space=(out_spaces or {}).get(i, pltpu.VMEM))
            for i in range(len(outs))
        ],
        scratch_shapes=list(scratch),
        compiler_params=pltpu.CompilerParams(vmem_limit_bytes=limit * MIB),
        cost_estimate=pl.CostEstimate(
            flops=flops, bytes_accessed=nbytes, transcendentals=transcendentals
        ),
    )(*args)


def shift(value, axis, step):
    size = lax.axis_size(axis)
    return lax.ppermute(value, axis, [(i, (i + step) % size) for i in range(size)])


def exchange(value):
    return lax.all_to_all(value, AXES, split_axis=0, concat_axis=0, tiled=True)


def shards(
    state,
    group_member,
    w_in,
    bias_in,
    w_mid,
    bias_mid,
    w_out,
    intersection_element,
    ocean_owner,
    ocean_block,
    regrid_weight,
):
    size_x, size_y, features = state.shape
    devices = lax.axis_size("gx") * lax.axis_size("gy")
    columns = size_x * size_y
    capacity = 2 * columns // devices
    slots = devices * capacity
    count = intersection_element.shape[0]
    line = ((size_x, features), F32)

    x_low, x_high, y_low, y_high = call(
        edges_kernel,
        [line] * 4,
        state,
        nbytes=2 * MIB,
        flops=MIB,
    )
    x_before, x_after = shift(x_high, "gx", 1), shift(x_low, "gx", -1)

    def local(token):
        return call(
            local_kernel,
            [(state.shape, F32)],
            state,
            token,
            nbytes=8 * MIB,
            flops=64 * MIB,
            spaces={1: pl.ANY},
            scratch=[pltpu.VMEM((size_x + 2, size_y, features), F32)],
        )[0]

    partial = local(x_low)
    slot_row, hot_rows, hot_sides = call(
        lambda *refs: route_kernel(capacity, size_y, *refs),
        [((1, columns), jnp.int32), ((slots, columns), BF16), ((slots, 128), BF16)],
        group_member.reshape(1, columns),
        nbytes=8 * MIB,
        flops=64 * MIB,
    )
    low, high = call(
        sides_kernel,
        [line] * 2,
        y_low,
        y_high,
        x_before,
        x_after,
        partial,
        slot_row,
        spaces={4: pl.ANY, 5: pl.ANY},
    )
    y_before, y_after = shift(high, "gy", 1), shift(low, "gy", -1)
    inner, sides = call(
        inner_kernel,
        [((slots, features), BF16), ((2 * size_x, features), F32)],
        partial,
        x_before,
        x_after,
        hot_rows,
        nbytes=8 * MIB,
        flops=2 * slots * columns * features,
        scratch=[pltpu.VMEM(state.shape, F32)],
    )
    (send,) = call(
        pack_kernel,
        [((slots, features), BF16)],
        inner,
        sides,
        y_before,
        y_after,
        hot_sides,
        nbytes=4 * MIB,
        flops=2 * slots * 128 * features,
        out_spaces={0: pl.ANY},
        scratch=[pltpu.VMEM((slots, features), BF16), pltpu.SemaphoreType.DMA((4,))],
    )
    received = exchange(send.reshape(devices, capacity, features)).reshape(slots, features)

    w_flux = jnp.tile(w_out[0, :, features:], (1, 16))
    hidden = w_in.shape[2]
    owner_row = ocean_owner.reshape(1, count)
    first, blocks = call(
        first_kernel,
        [((slots, hidden), BF16), ((devices, 128), F32)],
        received,
        w_in,
        bias_in,
        owner_row,
        ocean_block.reshape(1, count),
        nbytes=6 * MIB,
        flops=2 * slots * features * hidden,
        transcendentals=slots * hidden,
        scratch=[pltpu.VMEM((features, hidden), BF16)],
    )
    answered, token = call(
        second_kernel,
        [((devices, 40, 128), BF16), ((8, 128), F32)],
        first,
        w_mid,
        bias_mid,
        w_out,
        w_flux,
        blocks,
        nbytes=8 * MIB,
        flops=2 * slots * hidden * (hidden + 384),
        transcendentals=slots * hidden,
        limit=24,
        out_spaces={0: pl.ANY},
        scratch=[
            pltpu.VMEM((hidden, hidden), BF16),
            pltpu.VMEM((devices, 40, 128), BF16),
            pltpu.SemaphoreType.DMA((4,)),
        ],
    )
    answer = exchange(answered)
    places, tiled = call(
        lambda *refs: prepare_kernel(capacity, *refs),
        [((count, 128), jnp.int32), ((16, count, 128), F32)],
        intersection_element.reshape(1, count),
        regrid_weight,
        slot_row,
        token,
        nbytes=12 * MIB,
        flops=2 * 16 * count * columns * 256,
    )
    (ocean_send,) = call(
        lambda *refs: contribution_kernel(capacity, *refs),
        [((2 * devices, 128), F32)],
        answer,
        places,
        tiled,
        owner_row,
        nbytes=4 * MIB,
        flops=2 * 2 * 2048 * 128 * 128,
    )
    ocean_got = exchange(ocean_send.reshape(devices, 2, 128))
    partial = local(ocean_send)
    new_state, sums = call(
        columns_kernel,
        [(state.shape, F32), ((2, OB_DEV, devices), F32)],
        answer,
        slot_row,
        partial,
        x_before,
        x_after,
        y_before,
        y_after,
        nbytes=12 * MIB,
        flops=2 * slots * columns * features,
        scratch=[pltpu.VMEM((slots, features), BF16), pltpu.VMEM(state.shape, F32)],
    )
    (ocean_total,) = call(
        ocean_kernel, [((OB_DEV, 128), F32)], ocean_got, sums, nbytes=MIB, flops=MIB
    )
    return (new_state, ocean_total)


def solution(mesh):
    return jax.shard_map(
        shards,
        mesh=mesh,
        in_specs=(
            P("gx", "gy", None),
            P(("gx", "gy"), None),
            P(("gx", "gy"), None, None),
            P(("gx", "gy"), None),
            P(("gx", "gy"), None, None),
            P(("gx", "gy"), None),
            P(("gx", "gy"), None, None),
            P(("gx", "gy")),
            P(("gx", "gy"), None),
            P(("gx", "gy")),
            P(("gx", "gy"), None),
        ),
        out_specs=(P("gx", "gy", None), P(("gx", "gy"), None)),
        check_vma=False,
    )
```

```python
import math

import jax
import jax.numpy as jnp
import numpy as np
from jax import lax
from jax.experimental import pallas as pl
from jax.experimental.pallas import tpu as pltpu
from jax.sharding import PartitionSpec as P

LEV = 64
OB_DEV = 16
STEP_DT = 0.2
HIGHEST = lax.Precision.HIGHEST
AXES = ("gy", "gx")
F32 = jnp.float32
BF16 = jnp.bfloat16
MIB = 1 << 20


def derivative_table():
    root = 1.0 / math.sqrt(5.0)
    nodes = np.array([-1.0, -root, root, 1.0])
    table = np.zeros((4, 4))
    for row_index in range(4):
        for col_index in range(4):
            if row_index == col_index:
                table[row_index, col_index] = sum(
                    (
                        1.0 / (nodes[row_index] - nodes[other])
                        for other in range(4)
                        if other != row_index
                    )
                )
            else:
                weight_row = np.prod(
                    [nodes[row_index] - nodes[other] for other in range(4) if other != row_index]
                )
                weight_col = np.prod(
                    [nodes[col_index] - nodes[other] for other in range(4) if other != col_index]
                )
                table[row_index, col_index] = weight_row / (
                    weight_col * (nodes[row_index] - nodes[col_index])
                )
    return table


TABLE = [[float(np.float32(v)) for v in row] for row in derivative_table()]


def iota(shape, dim):
    return lax.broadcasted_iota(jnp.int32, shape, dim)


def dot(a, b, precision=None):
    return jnp.dot(a, b, preferred_element_type=F32, precision=precision)


def along_rows(line):
    rows, features = line.shape
    groups = line.reshape(rows // 8, 8, features)
    phase = iota((1, 8, features), 1) % 4
    total = None
    for offset in range(-3, 4):
        weight = jnp.zeros((1, 8, features), F32)
        for p in range(4):
            if 0 <= p + offset < 4:
                weight = jnp.where(phase == p, TABLE[p][p + offset], weight)
        moved = groups if offset == 0 else pltpu.roll(groups, (-offset) % 8, 1)
        total = weight * moved if total is None else total + weight * moved
    return total.reshape(rows, features)


def winds(line):
    pair = line[:, 128:]
    swapped = pltpu.roll(pair, LEV, 1)
    first = iota(pair.shape, 1) < LEV
    return jnp.where(first, pair, swapped), jnp.where(first, swapped, pair)


def advect(line, along_x, along_y):
    u, v = winds(line)
    return jnp.concatenate(
        [
            -(u * along_x[:, :128] + v * along_y[:, :128]),
            -(u * along_x[:, 128:] + v * along_y[:, 128:]),
        ],
        axis=1,
    )


def across(lines, i):
    total = TABLE[i][0] * lines[0]
    for j in range(1, 4):
        total = total + TABLE[i][j] * lines[j]
    return total


def smooth_rows(line):
    rows, features = line.shape
    row = iota((rows, features), 0)
    phase = row % 4
    before = jnp.where(row == 0, 0.0, pltpu.roll(line, 1, 0))
    after = jnp.where(row == rows - 1, 0.0, pltpu.roll(line, rows - 1, 0))
    return jnp.where(
        phase == 0,
        0.5 * (line + before),
        jnp.where(phase == 3, 0.5 * (line + after), line),
    )


def edges_kernel(state, x_low, x_high, y_low, y_high):
    size_x, size_y, _ = state.shape
    for out, base, i in ((x_low, 0, 0), (x_high, size_x - 4, 3)):
        lines = [state[base + j] for j in range(4)]
        out[...] = advect(lines[i], across(lines, i), along_rows(lines[i]))
    for out, base, i in ((y_low, 0, 0), (y_high, size_y - 4, 3)):
        lines = [state[:, base + j, :] for j in range(4)]
        out[...] = advect(lines[i], along_rows(lines[i]), across(lines, i))


def sides_kernel(y_low, y_high, x_before, x_after, partial, slot_row, low, high):
    size, features = y_low.shape
    row = iota((size, features), 0)
    for out, line, y in ((low, y_low, 0), (high, y_high, size - 1)):
        extra = jnp.where(
            row == 0,
            0.5 * x_before[y : y + 1, :],
            jnp.where(row == size - 1, 0.5 * x_after[y : y + 1, :], 0.0),
        )
        out[...] = smooth_rows(line[...]) + extra


def local_kernel(state, token, partial, tend):
    size_x, size_y, features = state.shape
    tend[0] = jnp.zeros((size_y, features), F32)
    tend[size_x + 1] = jnp.zeros((size_y, features), F32)

    @pl.loop(0, size_x // 4)
    def _(e):
        lines = [state[4 * e + j] for j in range(4)]
        for i in range(4):
            tend[4 * e + i + 1] = advect(lines[i], across(lines, i), along_rows(lines[i]))

    @pl.loop(0, size_x // 4)
    def _(e):
        low = 4 * e + 1
        values = [
            0.5 * (tend[low] + tend[low - 1]),
            tend[low + 1],
            tend[low + 2],
            0.5 * (tend[low + 3] + tend[low + 4]),
        ]
        for i in range(4):
            partial[4 * e + i] = state[4 * e + i] + STEP_DT * smooth_rows(values[i])


def owner_ranks(owners):
    count = owners.shape[1]
    earlier = (iota((count, count), 0) < iota((count, count), 1)).astype(F32).astype(BF16)
    hot = (iota((128, count), 0) == owners).astype(F32)
    rank = jnp.sum(dot(hot.astype(BF16), earlier) * hot, axis=0, keepdims=True)
    return hot, rank.astype(jnp.int32)


def position(device, sizes):
    size_gx, size_gy = sizes
    return device % size_gy * size_gx + device // size_gy


def route_kernel(sizes, capacity, size_y, member_row, slot_row, hot_rows, hot_sides):
    columns = member_row.shape[1]
    size_x = columns // size_y
    earlier = (iota((128, 128), 0) < iota((128, 128), 1)).astype(F32).astype(BF16)
    seen = jnp.zeros((128, 1), F32)
    for b in range(columns // 128):
        part = slice(b * 128, (b + 1) * 128)
        members = position(member_row[:, part], sizes)
        hot = (iota((128, 128), 0) == members).astype(F32)
        count = dot(hot.astype(BF16), earlier) + seen
        rank = jnp.sum(count * hot, axis=0, keepdims=True).astype(jnp.int32)
        slot_row[:, part] = members * capacity + rank
        seen = seen + jnp.sum(hot, axis=1, keepdims=True)
    step = 256
    slots = slot_row[...]
    for b in range(hot_rows.shape[0] // step):
        hot = iota((step, columns), 0) + b * step == slots
        hot_rows[b * step : (b + 1) * step, :] = hot.astype(F32).astype(BF16)
    lane = iota((columns, 128), 1)
    place = (lane % size_x) * size_y + (lane // size_x) * (size_y - 1)
    choose = ((iota((columns, 128), 0) == place) & (lane < 2 * size_x)).astype(F32).astype(BF16)
    row = iota((8, columns), 0)
    both = jnp.where(row == 0, slots // capacity, jnp.where(row == 1, slots % capacity, 0))
    both = dot(both.astype(F32).astype(BF16), choose).astype(jnp.int32)
    side = both[0:1, :] * capacity + both[1:2, :]
    side = jnp.where(iota((1, 128), 1) < 2 * size_x, side, -1)
    for b in range(hot_sides.shape[0] // step):
        hot = iota((step, 128), 0) + b * step == side
        hot_sides[b * step : (b + 1) * step, :] = hot.astype(F32).astype(BF16)


def add_before_after(advanced, partial, x_before, x_after):
    size_x, _, _ = partial.shape
    advanced[...] = partial[...]
    half = 0.5 * STEP_DT
    advanced[0] = advanced[0] + half * smooth_rows(x_before[...])
    advanced[size_x - 1] = advanced[size_x - 1] + half * smooth_rows(x_after[...])


def inner_kernel(partial, x_before, x_after, hot_rows, send, sides, advanced):
    size_x, size_y, features = partial.shape
    add_before_after(advanced, partial, x_before, x_after)
    for i, y in enumerate((0, size_y - 1)):
        sides[i * size_x : (i + 1) * size_x, :] = advanced[:, y, :]
        advanced[:, y, :] = jnp.zeros((size_x, features), F32)
    columns = advanced[...].reshape(size_x * size_y, features).astype(BF16)
    step = 256
    for b in range(send.shape[0] // step):
        part = slice(b * step, (b + 1) * step)
        send[part, :] = dot(hot_rows[part, :], columns).astype(BF16)


def pack_kernel(inner, sides, y_before, y_after, hot_sides, send_out, send, sems):
    half = 0.5 * STEP_DT
    size, features = y_before.shape
    columns = jnp.concatenate(
        [
            sides[0:size, :] + half * y_before[...],
            sides[size : 2 * size, :] + half * y_after[...],
            jnp.zeros((128 - 2 * size, features), F32),
        ],
        axis=0,
    ).astype(BF16)
    step = send.shape[0] // sems.shape[0]
    copies = []
    for b in range(sems.shape[0]):
        part = slice(b * step, (b + 1) * step)
        send[part, :] = inner[part, :] + dot(hot_sides[part, :], columns).astype(BF16)
        copy = pltpu.make_async_copy(send.at[part], send_out.at[part], sems.at[b])
        copy.start()
        copies.append(copy)
    for copy in copies:
        copy.wait()


def as_column(row):
    wide = jnp.where(iota((128, 128), 0) == iota((128, 128), 1), row, 0)
    return jnp.sum(wide, axis=1, keepdims=True)


def prepare_kernel(capacity, element_row, weight, slot_row, places, tiled):
    count = element_row.shape[1]
    lane = iota((count, 128), 1)
    for c in range(8):
        part = weight[:, (c // 4) * 128 : (c // 4 + 1) * 128]
        low = jnp.where(lane // 16 == 2 * c % 8, part, 0.0)
        high = jnp.where(lane // 16 == 2 * c % 8 + 1, part, 0.0)
        for distance in (64, 32, 16):
            low = low + pltpu.roll(low, distance, 1)
            high = high + pltpu.roll(high, distance, 1)
        tiled[c] = jnp.where(lane < 64, low, high)

    columns = slot_row.shape[1]
    lane = iota((128, 128), 1)
    table = []
    for b in range(columns // 128):
        slots = as_column(slot_row[:, b * 128 : (b + 1) * 128])
        both = jnp.where(lane == 0, slots // capacity, jnp.where(lane == 1, slots % capacity, 0))
        table.append(both.astype(F32).astype(BF16))
    table = jnp.concatenate(table, axis=0)
    element = as_column(element_row[...])
    base = (element // 8) * 128 + (element % 8) * 4
    place = iota((count, columns), 1)
    slots = jnp.zeros((count, 128), F32)
    for c in range(16):
        hot = (place == base + (c // 4) * 32 + c % 4).astype(F32).astype(BF16)
        both = dot(hot, table)
        slots = jnp.where(lane == c, both[:, 0:1] * capacity + both[:, 1:2], slots)
    places[...] = slots.astype(jnp.int32)


def silu_of_half(half):
    return half + half * jnp.tanh(half)


def first_kernel(sizes, rows, w_in, b_in, owner_row, block_row, places, out, blocks, w_half):
    owners = position(owner_row[...], sizes)
    hot, rank = owner_ranks(owners)
    values = block_row[...].astype(F32)
    lane = iota(blocks.shape, 1)
    first = jnp.sum(jnp.where(rank == 0, hot, 0.0) * values, axis=1, keepdims=True)
    second = jnp.sum(jnp.where(rank == 1, hot, 0.0) * values, axis=1, keepdims=True)
    blocks[...] = jnp.where(lane == 0, first, jnp.where(lane == 1, second, 0.0))

    w_half[...] = w_in[0] * jnp.asarray(0.5, BF16)
    b_half = 0.5 * b_in[...]
    step = 512
    for b in range(rows.shape[0] // step):
        part = slice(b * step, (b + 1) * step)
        out[part, :] = silu_of_half(dot(rows[part, :], w_half[...]) + b_half).astype(BF16)


def dot_by_output(a, b):
    return lax.dot_general(a, b, (((1,), (1,)), ((), ())), preferred_element_type=F32)


def second_kernel(first, w_mid, b_mid, w_last, blocks, out, w_half, w_flux):
    step = 512
    sources = step // 16
    lane = iota((step, 128), 1)
    own = lane // 8 == iota((step, 128), 0) % 16
    line = iota((sources, 8, 128), 1)
    w_half[...] = w_mid[0] * jnp.asarray(0.5, BF16)
    w_flux[...] = jnp.concatenate([w_last[0, 256:264, :].astype(F32)] * 16).astype(BF16)
    b_half = 0.5 * b_mid[...]
    for b in range(first.shape[0] // step):
        hidden = dot(first[b * step : (b + 1) * step, :], w_half[...])
        hidden = silu_of_half(hidden + b_half).astype(BF16)
        tends = dot_by_output(hidden, w_last[0, 0:256, :]).astype(BF16)
        part = slice(b * sources, (b + 1) * sources)
        out[part, 0:16, :] = tends[:, :128].reshape(sources, 16, 128)
        out[part, 16:32, :] = tends[:, 128:].reshape(sources, 16, 128)
        flux = jnp.where(own, dot_by_output(hidden, w_flux[...]), 0.0)
        flux = jnp.sum(flux.reshape(sources, 16, 128), axis=1, keepdims=True)
        names = blocks[part, :].reshape(sources, 1, 128)
        tail = jnp.where(line == 0, flux, jnp.where(line == 1, names, 0.0))
        out[part, 32:40, :] = tail.astype(BF16)


def contribution_kernel(sizes, capacity, answer, places, tiled, owner_row, send):
    flux = answer[:, 32:40, :].astype(F32)[:, 0, :].astype(BF16)
    spread = (iota((128, 128), 0) % 8 == iota((128, 128), 1) // 16).astype(F32).astype(BF16)
    lane = iota((128, 128), 1)
    total = None
    for c in range(16):
        if c % 2 == 0:
            pair = tiled[c // 2]
            swapped = pltpu.roll(pair, 64, 1)
        weights = jnp.where(lane < 64, *((pair, swapped) if c % 2 == 0 else (swapped, pair)))
        slots = places[:, c : c + 1]
        pick = (lane == slots // capacity).astype(F32).astype(BF16)
        value = jnp.where(lane // 8 == slots % capacity, dot(pick, flux), 0.0)
        term = dot(value.astype(BF16), spread) * weights
        total = term if total is None else total + term
    owners = position(owner_row[...], sizes)
    _, rank = owner_ranks(owners)
    hot = (iota(send.shape, 0) == owners * 2 + rank).astype(F32)
    send[...] = dot(hot, total, HIGHEST)


def columns_kernel(
    answer,
    slot_row,
    partial,
    x_before,
    x_after,
    y_before,
    y_after,
    new_state,
    sums,
    rows,
    advanced,
):
    sources = answer.shape[0]
    slots = sources * 16
    size_x, size_y, features = partial.shape
    add_before_after(advanced, partial, x_before, x_after)
    half = 0.5 * STEP_DT
    advanced[:, 0, :] = advanced[:, 0, :] + half * y_before[...]
    advanced[:, size_y - 1, :] = advanced[:, size_y - 1, :] + half * y_after[...]
    rows[:, 0:128] = answer[:, 0:16, :].reshape(slots, 128)
    rows[:, 128:256] = answer[:, 16:32, :].reshape(slots, 128)
    step = 128
    lines = step // size_y
    for b in range(size_x // lines):
        hot = iota((step, slots), 1) == as_column(slot_row[:, b * step : (b + 1) * step])
        tends = dot(hot.astype(F32).astype(BF16), rows[...])
        part = slice(b * lines, (b + 1) * lines)
        new_state[part] = advanced[part] + tends.reshape(lines, size_y, features)
    names = answer[:, 32:40, :].astype(F32)[:, 1, :]
    lane = iota((sources, 128), 1)
    for j in range(2):
        hot = (names[:, j : j + 1].astype(jnp.int32) == lane).astype(F32)
        sums[j] = jnp.transpose(hot)[:OB_DEV, :]


def ocean_kernel(received, sums, out):
    out[...] = dot(sums[0], received[:, 0, :], HIGHEST) + dot(sums[1], received[:, 1, :], HIGHEST)


def call(kernel, outs, *args, flops=0, nbytes=0, transcendentals=0, scratch=(), limit=16, spaces=None, out_spaces=None):
    return pl.pallas_call(
        kernel,
        out_shape=[jax.ShapeDtypeStruct(s, d) for s, d in outs],
        in_specs=[
            pl.BlockSpec(memory_space=(spaces or {}).get(i, pltpu.VMEM)) for i in range(len(args))
        ],
        out_specs=[
            pl.BlockSpec(memory_space=(out_spaces or {}).get(i, pltpu.VMEM))
            for i in range(len(outs))
        ],
        scratch_shapes=list(scratch),
        compiler_params=pltpu.CompilerParams(vmem_limit_bytes=limit * MIB),
        cost_estimate=pl.CostEstimate(
            flops=flops, bytes_accessed=nbytes, transcendentals=transcendentals
        ),
    )(*args)


def shift(value, axis, step):
    size = lax.axis_size(axis)
    return lax.ppermute(value, axis, [(i, (i + step) % size) for i in range(size)])


def exchange(value):
    return lax.all_to_all(value, AXES, split_axis=0, concat_axis=0, tiled=True)


def shards(
    state,
    group_member,
    w_in,
    bias_in,
    w_mid,
    bias_mid,
    w_out,
    intersection_element,
    ocean_owner,
    ocean_block,
    regrid_weight,
):
    size_x, size_y, features = state.shape
    sizes = lax.axis_size("gx"), lax.axis_size("gy")
    devices = sizes[0] * sizes[1]
    columns = size_x * size_y
    capacity = 2 * columns // devices
    slots = devices * capacity
    count = intersection_element.shape[0]
    line = ((size_x, features), F32)

    x_low, x_high, y_low, y_high = call(
        edges_kernel,
        [line] * 4,
        state,
        nbytes=2 * MIB,
        flops=MIB,
    )
    x_before, x_after = shift(x_high, "gx", 1), shift(x_low, "gx", -1)

    def local(token):
        return call(
            local_kernel,
            [(state.shape, F32)],
            state,
            token,
            nbytes=8 * MIB,
            flops=64 * MIB,
            spaces={1: pl.ANY},
            scratch=[pltpu.VMEM((size_x + 2, size_y, features), F32)],
        )[0]

    partial = local(x_low)
    slot_row, hot_rows, hot_sides = call(
        lambda *refs: route_kernel(sizes, capacity, size_y, *refs),
        [((1, columns), jnp.int32), ((slots, columns), BF16), ((slots, 128), BF16)],
        group_member.reshape(1, columns),
        nbytes=8 * MIB,
        flops=64 * MIB,
    )
    low, high = call(
        sides_kernel,
        [line] * 2,
        y_low,
        y_high,
        x_before,
        x_after,
        partial,
        slot_row,
        spaces={4: pl.ANY, 5: pl.ANY},
    )
    y_before, y_after = shift(high, "gy", 1), shift(low, "gy", -1)
    inner, sides = call(
        inner_kernel,
        [((slots, features), BF16), ((2 * size_x, features), F32)],
        partial,
        x_before,
        x_after,
        hot_rows,
        nbytes=8 * MIB,
        flops=2 * slots * columns * features,
        scratch=[pltpu.VMEM(state.shape, F32)],
    )
    (send,) = call(
        pack_kernel,
        [((slots, features), BF16)],
        inner,
        sides,
        y_before,
        y_after,
        hot_sides,
        nbytes=4 * MIB,
        flops=2 * slots * 128 * features,
        out_spaces={0: pl.ANY},
        scratch=[pltpu.VMEM((slots, features), BF16), pltpu.SemaphoreType.DMA((4,))],
    )
    received = exchange(send.reshape(devices, capacity, features)).reshape(slots, features)

    places, tiled = call(
        lambda *refs: prepare_kernel(capacity, *refs),
        [((count, 128), jnp.int32), ((8, count, 128), F32)],
        intersection_element.reshape(1, count),
        regrid_weight,
        slot_row,
        nbytes=12 * MIB,
        flops=2 * 16 * count * columns * 256,
    )
    hidden = w_in.shape[2]
    owner_row = ocean_owner.reshape(1, count)
    first, blocks = call(
        lambda *refs: first_kernel(sizes, *refs),
        [((slots, hidden), BF16), ((devices, 128), F32)],
        received,
        w_in,
        bias_in,
        owner_row,
        ocean_block.reshape(1, count),
        places,
        spaces={5: pl.ANY},
        nbytes=6 * MIB,
        flops=2 * slots * features * hidden,
        transcendentals=slots * hidden,
        scratch=[pltpu.VMEM((features, hidden), BF16)],
    )
    (answered,) = call(
        second_kernel,
        [((devices, 40, 128), BF16)],
        first,
        w_mid,
        bias_mid,
        jnp.swapaxes(w_out, 1, 2),
        blocks,
        nbytes=8 * MIB,
        flops=2 * slots * hidden * (hidden + 384),
        transcendentals=slots * hidden,
        limit=24,
        scratch=[pltpu.VMEM((hidden, hidden), BF16), pltpu.VMEM((128, hidden), BF16)],
    )
    answer = exchange(answered)
    (ocean_send,) = call(
        lambda *refs: contribution_kernel(sizes, capacity, *refs),
        [((2 * devices, 128), F32)],
        answer,
        places,
        tiled,
        owner_row,
        nbytes=4 * MIB,
        flops=2 * 2 * 2048 * 128 * 128,
    )
    ocean_got = exchange(ocean_send.reshape(devices, 2, 128))
    partial = local(ocean_send)
    new_state, sums = call(
        columns_kernel,
        [(state.shape, F32), ((2, OB_DEV, devices), F32)],
        answer,
        slot_row,
        partial,
        x_before,
        x_after,
        y_before,
        y_after,
        nbytes=12 * MIB,
        flops=2 * slots * columns * features,
        scratch=[pltpu.VMEM((slots, features), BF16), pltpu.VMEM(state.shape, F32)],
    )
    (ocean_total,) = call(
        ocean_kernel, [((OB_DEV, 128), F32)], ocean_got, sums, nbytes=MIB, flops=MIB
    )
    return (new_state, ocean_total)


def solution(mesh):
    return jax.shard_map(
        shards,
        mesh=mesh,
        in_specs=(
            P("gx", "gy", None),
            P(("gx", "gy"), None),
            P(("gx", "gy"), None, None),
            P(("gx", "gy"), None),
            P(("gx", "gy"), None, None),
            P(("gx", "gy"), None),
            P(("gx", "gy"), None, None),
            P(("gx", "gy")),
            P(("gx", "gy"), None),
            P(("gx", "gy")),
            P(("gx", "gy"), None),
        ),
        out_specs=(P("gx", "gy", None), P(("gx", "gy"), None)),
        check_vma=False,
    )
```

```python
import math

import jax
import jax.numpy as jnp
import numpy as np
from jax import lax
from jax.experimental import pallas as pl
from jax.experimental.pallas import tpu as pltpu
from jax.sharding import PartitionSpec as P

LEV = 64
OB_DEV = 16
STEP_DT = 0.2
HIGHEST = lax.Precision.HIGHEST
AXES = ("gy", "gx")
F32 = jnp.float32
BF16 = jnp.bfloat16
MIB = 1 << 20


def derivative_table():
    root = 1.0 / math.sqrt(5.0)
    nodes = np.array([-1.0, -root, root, 1.0])
    table = np.zeros((4, 4))
    for row_index in range(4):
        for col_index in range(4):
            if row_index == col_index:
                table[row_index, col_index] = sum(
                    (
                        1.0 / (nodes[row_index] - nodes[other])
                        for other in range(4)
                        if other != row_index
                    )
                )
            else:
                weight_row = np.prod(
                    [nodes[row_index] - nodes[other] for other in range(4) if other != row_index]
                )
                weight_col = np.prod(
                    [nodes[col_index] - nodes[other] for other in range(4) if other != col_index]
                )
                table[row_index, col_index] = weight_row / (
                    weight_col * (nodes[row_index] - nodes[col_index])
                )
    return table


TABLE = [[float(np.float32(v)) for v in row] for row in derivative_table()]


def iota(shape, dim):
    return lax.broadcasted_iota(jnp.int32, shape, dim)


def dot(a, b, precision=None):
    return jnp.dot(a, b, preferred_element_type=F32, precision=precision)


def along_rows(line):
    rows, features = line.shape
    groups = line.reshape(rows // 8, 8, features)
    phase = iota((1, 8, features), 1) % 4
    total = None
    for offset in range(-3, 4):
        weight = jnp.zeros((1, 8, features), F32)
        for p in range(4):
            if 0 <= p + offset < 4:
                weight = jnp.where(phase == p, TABLE[p][p + offset], weight)
        moved = groups if offset == 0 else pltpu.roll(groups, (-offset) % 8, 1)
        total = weight * moved if total is None else total + weight * moved
    return total.reshape(rows, features)


def winds(line):
    pair = line[:, 128:]
    swapped = pltpu.roll(pair, LEV, 1)
    first = iota(pair.shape, 1) < LEV
    return jnp.where(first, pair, swapped), jnp.where(first, swapped, pair)


def advect(line, along_x, along_y):
    u, v = winds(line)
    return jnp.concatenate(
        [
            -(u * along_x[:, :128] + v * along_y[:, :128]),
            -(u * along_x[:, 128:] + v * along_y[:, 128:]),
        ],
        axis=1,
    )


def across(lines, i):
    total = TABLE[i][0] * lines[0]
    for j in range(1, 4):
        total = total + TABLE[i][j] * lines[j]
    return total


def smooth_rows(line):
    rows, features = line.shape
    row = iota((rows, features), 0)
    phase = row % 4
    before = jnp.where(row == 0, 0.0, pltpu.roll(line, 1, 0))
    after = jnp.where(row == rows - 1, 0.0, pltpu.roll(line, rows - 1, 0))
    return jnp.where(
        phase == 0,
        0.5 * (line + before),
        jnp.where(phase == 3, 0.5 * (line + after), line),
    )


def edges_kernel(state, x_low, x_high, y_low, y_high):
    size_x, size_y, _ = state.shape
    for out, base, i in ((x_low, 0, 0), (x_high, size_x - 4, 3)):
        lines = [state[base + j] for j in range(4)]
        out[...] = advect(lines[i], across(lines, i), along_rows(lines[i]))
    for out, base, i in ((y_low, 0, 0), (y_high, size_y - 4, 3)):
        lines = [state[:, base + j, :] for j in range(4)]
        out[...] = advect(lines[i], along_rows(lines[i]), across(lines, i))


def sides_kernel(y_low, y_high, x_before, x_after, partial, slot_row, low, high):
    size, features = y_low.shape
    row = iota((size, features), 0)
    for out, line, y in ((low, y_low, 0), (high, y_high, size - 1)):
        extra = jnp.where(
            row == 0,
            0.5 * x_before[y : y + 1, :],
            jnp.where(row == size - 1, 0.5 * x_after[y : y + 1, :], 0.0),
        )
        out[...] = smooth_rows(line[...]) + extra


def local_kernel(state, token, partial, tend):
    size_x, size_y, features = state.shape
    tend[0] = jnp.zeros((size_y, features), F32)
    tend[size_x + 1] = jnp.zeros((size_y, features), F32)

    @pl.loop(0, size_x // 4)
    def _(e):
        lines = [state[4 * e + j] for j in range(4)]
        for i in range(4):
            tend[4 * e + i + 1] = advect(lines[i], across(lines, i), along_rows(lines[i]))

    @pl.loop(0, size_x // 4)
    def _(e):
        low = 4 * e + 1
        values = [
            0.5 * (tend[low] + tend[low - 1]),
            tend[low + 1],
            tend[low + 2],
            0.5 * (tend[low + 3] + tend[low + 4]),
        ]
        for i in range(4):
            partial[4 * e + i] = state[4 * e + i] + STEP_DT * smooth_rows(values[i])


def dot_parts(hot, values):
    total = None
    for _ in range(3):
        part = values.astype(BF16)
        term = dot(hot, part)
        total = term if total is None else total + term
        values = values - part.astype(F32)
    return total


def owner_ranks(owners):
    count = owners.shape[1]
    earlier = (iota((count, count), 0) < iota((count, count), 1)).astype(F32).astype(BF16)
    hot = (iota((128, count), 0) == owners).astype(F32)
    rank = jnp.sum(dot(hot.astype(BF16), earlier) * hot, axis=0, keepdims=True)
    return hot, rank.astype(jnp.int32)


def position(device, sizes):
    size_gx, size_gy = sizes
    return device % size_gy * size_gx + device // size_gy


def route_kernel(sizes, capacity, size_y, member_row, slot_row, hot_rows, hot_sides):
    columns = member_row.shape[1]
    size_x = columns // size_y
    earlier = (iota((128, 128), 0) < iota((128, 128), 1)).astype(F32).astype(BF16)
    seen = jnp.zeros((128, 1), F32)
    for b in range(columns // 128):
        part = slice(b * 128, (b + 1) * 128)
        members = position(member_row[:, part], sizes)
        hot = (iota((128, 128), 0) == members).astype(F32)
        count = dot(hot.astype(BF16), earlier) + seen
        rank = jnp.sum(count * hot, axis=0, keepdims=True).astype(jnp.int32)
        slot_row[:, part] = members * capacity + rank
        seen = seen + jnp.sum(hot, axis=1, keepdims=True)
    step = 256
    slots = slot_row[...]
    for b in range(hot_rows.shape[0] // step):
        hot = iota((step, columns), 0) + b * step == slots
        hot_rows[b * step : (b + 1) * step, :] = hot.astype(F32).astype(BF16)
    lane = iota((columns, 128), 1)
    place = (lane % size_x) * size_y + (lane // size_x) * (size_y - 1)
    choose = ((iota((columns, 128), 0) == place) & (lane < 2 * size_x)).astype(F32).astype(BF16)
    row = iota((8, columns), 0)
    both = jnp.where(row == 0, slots // capacity, jnp.where(row == 1, slots % capacity, 0))
    both = dot(both.astype(F32).astype(BF16), choose).astype(jnp.int32)
    side = both[0:1, :] * capacity + both[1:2, :]
    side = jnp.where(iota((1, 128), 1) < 2 * size_x, side, -1)
    for b in range(hot_sides.shape[0] // step):
        hot = iota((step, 128), 0) + b * step == side
        hot_sides[b * step : (b + 1) * step, :] = hot.astype(F32).astype(BF16)


def add_before_after(advanced, partial, x_before, x_after):
    size_x, _, _ = partial.shape
    advanced[...] = partial[...]
    half = 0.5 * STEP_DT
    advanced[0] = advanced[0] + half * smooth_rows(x_before[...])
    advanced[size_x - 1] = advanced[size_x - 1] + half * smooth_rows(x_after[...])


def inner_kernel(partial, x_before, x_after, hot_rows, send, sides, advanced):
    size_x, size_y, features = partial.shape
    add_before_after(advanced, partial, x_before, x_after)
    for i, y in enumerate((0, size_y - 1)):
        sides[i * size_x : (i + 1) * size_x, :] = advanced[:, y, :]
        advanced[:, y, :] = jnp.zeros((size_x, features), F32)
    columns = advanced[...].reshape(size_x * size_y, features).astype(BF16)
    step = 256
    for b in range(send.shape[0] // step):
        part = slice(b * step, (b + 1) * step)
        send[part, :] = dot(hot_rows[part, :], columns).astype(BF16)


def pack_kernel(inner, sides, y_before, y_after, hot_sides, members, send):
    half = 0.5 * STEP_DT
    size, features = y_before.shape
    columns = jnp.concatenate(
        [
            sides[0:size, :] + half * y_before[...],
            sides[size : 2 * size, :] + half * y_after[...],
            jnp.zeros((128 - 2 * size, features), F32),
        ],
        axis=0,
    ).astype(BF16)
    step = 512
    for b in range(send.shape[0] // step):
        part = slice(b * step, (b + 1) * step)
        send[part, :] = inner[part, :] + dot(hot_sides[part, :], columns).astype(BF16)


def as_column(row):
    wide = jnp.where(iota((128, 128), 0) == iota((128, 128), 1), row, 0)
    return jnp.sum(wide, axis=1, keepdims=True)


def prepare_kernel(capacity, size_y, element_row, weight, slot_row, sides, members, ranks, tiled):
    count = element_row.shape[1]
    lane = iota((count, 128), 1)
    for c in range(8):
        part = weight[:, (c // 4) * 128 : (c // 4 + 1) * 128]
        low = jnp.where(lane // 16 == 2 * c % 8, part, 0.0)
        high = jnp.where(lane // 16 == 2 * c % 8 + 1, part, 0.0)
        for distance in (64, 32, 16):
            low = low + pltpu.roll(low, distance, 1)
            high = high + pltpu.roll(high, distance, 1)
        tiled[c] = jnp.where(lane < 64, low, high)

    columns = slot_row.shape[1]
    elements_y = size_y // 4
    table = []
    for b in range(columns // 128):
        slots = as_column(slot_row[:, b * 128 : (b + 1) * 128])
        column = iota((128, 128), 0) + b * 128
        here = column // size_y % 4 * 4 + column % 4 == lane
        member = jnp.where(here, slots // capacity, 0).astype(F32)
        rank = jnp.where(here, slots % capacity, 0).astype(F32)
        table.append(jnp.concatenate([member, rank], axis=1).astype(BF16))
    column = iota((128, columns), 1)
    element = column // (4 * size_y) * elements_y + column % size_y // 4
    hot = (iota((128, columns), 0) == element).astype(F32).astype(BF16)
    by_element = dot(hot, jnp.concatenate(table, axis=0)).astype(BF16)
    hot = (lane == as_column(element_row[...])).astype(F32).astype(BF16)
    both = dot(hot, by_element)
    members[...] = both[:, :128].astype(jnp.int32)
    ranks[...] = both[:, 128:].astype(jnp.int32)


def silu_of_half(half):
    return half + half * jnp.tanh(half)


def first_kernel(sizes, rows, w_in, b_in, owner_row, block_row, out, blocks, w_half):
    owners = position(owner_row[...], sizes)
    hot, rank = owner_ranks(owners)
    values = block_row[...].astype(F32)
    lane = iota(blocks.shape, 1)
    first = jnp.sum(jnp.where(rank == 0, hot, 0.0) * values, axis=1, keepdims=True)
    second = jnp.sum(jnp.where(rank == 1, hot, 0.0) * values, axis=1, keepdims=True)
    blocks[...] = jnp.where(lane == 0, first, jnp.where(lane == 1, second, 0.0))

    w_half[...] = w_in[0] * jnp.asarray(0.5, BF16)
    b_half = 0.5 * b_in[...]
    step = 512
    for b in range(rows.shape[0] // step):
        part = slice(b * step, (b + 1) * step)
        out[part, :] = silu_of_half(dot(rows[part, :], w_half[...]) + b_half).astype(BF16)


def dot_by_output(a, b):
    return lax.dot_general(a, b, (((1,), (1,)), ((), ())), preferred_element_type=F32)


def second_kernel(first, w_mid, b_mid, w_last, blocks, out, w_half, w_flux):
    step = 512
    sources = step // 16
    lane = iota((step, 128), 1)
    own = lane // 8 == iota((step, 128), 0) % 16
    line = iota((sources, 8, 128), 1)
    w_half[...] = w_mid[0] * jnp.asarray(0.5, BF16)
    w_flux[...] = jnp.concatenate([w_last[0, 256:264, :].astype(F32)] * 16).astype(BF16)
    b_half = 0.5 * b_mid[...]
    for b in range(first.shape[0] // step):
        hidden = dot(first[b * step : (b + 1) * step, :], w_half[...])
        hidden = silu_of_half(hidden + b_half).astype(BF16)
        tends = dot_by_output(hidden, w_last[0, 0:256, :]).astype(BF16)
        part = slice(b * sources, (b + 1) * sources)
        out[part, 0:16, :] = tends[:, :128].reshape(sources, 16, 128)
        out[part, 16:32, :] = tends[:, 128:].reshape(sources, 16, 128)
        flux = jnp.where(own, dot_by_output(hidden, w_flux[...]), 0.0)
        flux = jnp.sum(flux.reshape(sources, 16, 128), axis=1, keepdims=True)
        names = blocks[part, :].reshape(sources, 1, 128)
        tail = jnp.where(line == 0, flux, jnp.where(line == 1, names, 0.0))
        out[part, 32:40, :] = tail.astype(BF16)


def contribution_kernel(sizes, answer, members, ranks, tiled, owner_row, send):
    flux = answer[:, 32:40, :].astype(F32)[:, 0, :].astype(BF16)
    spread = (iota((128, 128), 0) % 8 == iota((128, 128), 1) // 16).astype(F32).astype(BF16)
    lane = iota((128, 128), 1)
    group = lane // 8
    owners = position(owner_row[...], sizes)
    _, rank = owner_ranks(owners)
    hot = (iota(send.shape, 0) == owners * 2 + rank).astype(F32).astype(BF16)
    total = None
    for c in range(16):
        if c % 2 == 0:
            pair = tiled[c // 2]
            swapped = pltpu.roll(pair, 64, 1)
        weights = jnp.where(lane < 64, *((pair, swapped) if c % 2 == 0 else (swapped, pair)))
        pick = (lane == members[:, c : c + 1]).astype(F32).astype(BF16)
        value = jnp.where(group == ranks[:, c : c + 1], dot(pick, flux), 0.0)
        term = dot(value.astype(BF16), spread) * weights
        total = term if total is None else total + term
    send[...] = dot_parts(hot, total)


def columns_kernel(
    answer,
    slot_row,
    partial,
    x_before,
    x_after,
    y_before,
    y_after,
    new_state,
    sums,
    rows,
    advanced,
):
    sources = answer.shape[0]
    slots = sources * 16
    size_x, size_y, features = partial.shape
    add_before_after(advanced, partial, x_before, x_after)
    half = 0.5 * STEP_DT
    advanced[:, 0, :] = advanced[:, 0, :] + half * y_before[...]
    advanced[:, size_y - 1, :] = advanced[:, size_y - 1, :] + half * y_after[...]
    rows[:, 0:128] = answer[:, 0:16, :].reshape(slots, 128)
    rows[:, 128:256] = answer[:, 16:32, :].reshape(slots, 128)
    step = 128
    lines = step // size_y
    for b in range(size_x // lines):
        hot = iota((step, slots), 1) == as_column(slot_row[:, b * step : (b + 1) * step])
        tends = dot(hot.astype(F32).astype(BF16), rows[...])
        part = slice(b * lines, (b + 1) * lines)
        new_state[part] = advanced[part] + tends.reshape(lines, size_y, features)
    names = answer[:, 32:40, :].astype(F32)[:, 1, :]
    lane = iota((sources, 128), 1)
    for j in range(2):
        hot = (names[:, j : j + 1].astype(jnp.int32) == lane).astype(F32)
        sums[j] = jnp.transpose(hot)[:OB_DEV, :]


def ocean_kernel(received, sums, out):
    out[...] = dot(sums[0], received[:, 0, :], HIGHEST) + dot(sums[1], received[:, 1, :], HIGHEST)


def call(kernel, outs, *args, flops=0, nbytes=0, transcendentals=0, scratch=(), limit=16, spaces=None, out_spaces=None):
    return pl.pallas_call(
        kernel,
        out_shape=[jax.ShapeDtypeStruct(s, d) for s, d in outs],
        in_specs=[
            pl.BlockSpec(memory_space=(spaces or {}).get(i, pltpu.VMEM)) for i in range(len(args))
        ],
        out_specs=[
            pl.BlockSpec(memory_space=(out_spaces or {}).get(i, pltpu.VMEM))
            for i in range(len(outs))
        ],
        scratch_shapes=list(scratch),
        compiler_params=pltpu.CompilerParams(vmem_limit_bytes=limit * MIB),
        cost_estimate=pl.CostEstimate(
            flops=flops, bytes_accessed=nbytes, transcendentals=transcendentals
        ),
    )(*args)


def shift(value, axis, step):
    size = lax.axis_size(axis)
    return lax.ppermute(value, axis, [(i, (i + step) % size) for i in range(size)])


def exchange(value):
    return lax.all_to_all(value, AXES, split_axis=0, concat_axis=0, tiled=True)


def shards(
    state,
    group_member,
    w_in,
    bias_in,
    w_mid,
    bias_mid,
    w_out,
    intersection_element,
    ocean_owner,
    ocean_block,
    regrid_weight,
):
    size_x, size_y, features = state.shape
    sizes = lax.axis_size("gx"), lax.axis_size("gy")
    devices = sizes[0] * sizes[1]
    columns = size_x * size_y
    capacity = 2 * columns // devices
    slots = devices * capacity
    count = intersection_element.shape[0]
    line = ((size_x, features), F32)

    x_low, x_high, y_low, y_high = call(
        edges_kernel,
        [line] * 4,
        state,
        nbytes=2 * MIB,
        flops=MIB,
    )
    x_before, x_after = shift(x_high, "gx", 1), shift(x_low, "gx", -1)

    def local(token):
        return call(
            local_kernel,
            [(state.shape, F32)],
            state,
            token,
            nbytes=8 * MIB,
            flops=64 * MIB,
            spaces={1: pl.ANY},
            scratch=[pltpu.VMEM((size_x + 2, size_y, features), F32)],
        )[0]

    partial = local(x_low)
    slot_row, hot_rows, hot_sides = call(
        lambda *refs: route_kernel(sizes, capacity, size_y, *refs),
        [((1, columns), jnp.int32), ((slots, columns), BF16), ((slots, 128), BF16)],
        group_member.reshape(1, columns),
        nbytes=8 * MIB,
        flops=64 * MIB,
    )
    low, high = call(
        sides_kernel,
        [line] * 2,
        y_low,
        y_high,
        x_before,
        x_after,
        partial,
        slot_row,
        spaces={4: pl.ANY, 5: pl.ANY},
    )
    y_before, y_after = shift(high, "gy", 1), shift(low, "gy", -1)
    inner, sides = call(
        inner_kernel,
        [((slots, features), BF16), ((2 * size_x, features), F32)],
        partial,
        x_before,
        x_after,
        hot_rows,
        nbytes=8 * MIB,
        flops=2 * slots * columns * features,
        scratch=[pltpu.VMEM(state.shape, F32)],
    )
    members, ranks, tiled = call(
        lambda *refs: prepare_kernel(capacity, size_y, *refs),
        [((count, 128), jnp.int32)] * 2 + [((8, count, 128), F32)],
        intersection_element.reshape(1, count),
        regrid_weight,
        slot_row,
        sides,
        spaces={3: pl.ANY},
        nbytes=12 * MIB,
        flops=2 * 16 * count * columns * 256,
    )
    (send,) = call(
        pack_kernel,
        [((slots, features), BF16)],
        inner,
        sides,
        y_before,
        y_after,
        hot_sides,
        members,
        nbytes=4 * MIB,
        flops=2 * slots * 128 * features,
        spaces={5: pl.ANY},
    )
    received = exchange(send.reshape(devices, capacity, features)).reshape(slots, features)

    hidden = w_in.shape[2]
    owner_row = ocean_owner.reshape(1, count)
    first, blocks = call(
        lambda *refs: first_kernel(sizes, *refs),
        [((slots, hidden), BF16), ((devices, 128), F32)],
        received,
        w_in,
        bias_in,
        owner_row,
        ocean_block.reshape(1, count),
        nbytes=6 * MIB,
        flops=2 * slots * features * hidden,
        transcendentals=slots * hidden,
        scratch=[pltpu.VMEM((features, hidden), BF16)],
    )
    (answered,) = call(
        second_kernel,
        [((devices, 40, 128), BF16)],
        first,
        w_mid,
        bias_mid,
        jnp.swapaxes(w_out, 1, 2),
        blocks,
        nbytes=8 * MIB,
        flops=2 * slots * hidden * (hidden + 384),
        transcendentals=slots * hidden,
        limit=24,
        scratch=[pltpu.VMEM((hidden, hidden), BF16), pltpu.VMEM((128, hidden), BF16)],
    )
    answer = exchange(answered)
    (ocean_send,) = call(
        lambda *refs: contribution_kernel(sizes, *refs),
        [((2 * devices, 128), F32)],
        answer,
        members,
        ranks,
        tiled,
        owner_row,
        nbytes=4 * MIB,
        flops=2 * 2 * 2048 * 128 * 128,
    )
    ocean_got = exchange(ocean_send.reshape(devices, 2, 128))
    partial = local(ocean_send)
    new_state, sums = call(
        columns_kernel,
        [(state.shape, F32), ((2, OB_DEV, devices), F32)],
        answer,
        slot_row,
        partial,
        x_before,
        x_after,
        y_before,
        y_after,
        nbytes=12 * MIB,
        flops=2 * slots * columns * features,
        scratch=[pltpu.VMEM((slots, features), BF16), pltpu.VMEM(state.shape, F32)],
    )
    (ocean_total,) = call(
        ocean_kernel, [((OB_DEV, 128), F32)], ocean_got, sums, nbytes=MIB, flops=MIB
    )
    return (new_state, ocean_total)


def solution(mesh):
    return jax.shard_map(
        shards,
        mesh=mesh,
        in_specs=(
            P("gx", "gy", None),
            P(("gx", "gy"), None),
            P(("gx", "gy"), None, None),
            P(("gx", "gy"), None),
            P(("gx", "gy"), None, None),
            P(("gx", "gy"), None),
            P(("gx", "gy"), None, None),
            P(("gx", "gy")),
            P(("gx", "gy"), None),
            P(("gx", "gy")),
            P(("gx", "gy"), None),
        ),
        out_specs=(P("gx", "gy", None), P(("gx", "gy"), None)),
        check_vma=False,
    )
```

```python
import math

import jax
import jax.numpy as jnp
import numpy as np
from jax import lax
from jax.experimental import pallas as pl
from jax.experimental.pallas import tpu as pltpu
from jax.sharding import PartitionSpec as P

LEV = 64
OB_DEV = 16
STEP_DT = 0.2
HIGHEST = lax.Precision.HIGHEST
AXES = ("gy", "gx")
F32 = jnp.float32
BF16 = jnp.bfloat16
MIB = 1 << 20


def derivative_table():
    root = 1.0 / math.sqrt(5.0)
    nodes = np.array([-1.0, -root, root, 1.0])
    table = np.zeros((4, 4))
    for row_index in range(4):
        for col_index in range(4):
            if row_index == col_index:
                table[row_index, col_index] = sum(
                    (
                        1.0 / (nodes[row_index] - nodes[other])
                        for other in range(4)
                        if other != row_index
                    )
                )
            else:
                weight_row = np.prod(
                    [nodes[row_index] - nodes[other] for other in range(4) if other != row_index]
                )
                weight_col = np.prod(
                    [nodes[col_index] - nodes[other] for other in range(4) if other != col_index]
                )
                table[row_index, col_index] = weight_row / (
                    weight_col * (nodes[row_index] - nodes[col_index])
                )
    return table


TABLE = [[float(np.float32(v)) for v in row] for row in derivative_table()]


def iota(shape, dim):
    return lax.broadcasted_iota(jnp.int32, shape, dim)


def dot(a, b, precision=None):
    return jnp.dot(a, b, preferred_element_type=F32, precision=precision)


def along_rows(line):
    rows, features = line.shape
    groups = line.reshape(rows // 8, 8, features)
    phase = iota((1, 8, features), 1) % 4
    total = None
    for offset in range(-3, 4):
        weight = jnp.zeros((1, 8, features), F32)
        for p in range(4):
            if 0 <= p + offset < 4:
                weight = jnp.where(phase == p, TABLE[p][p + offset], weight)
        moved = groups if offset == 0 else pltpu.roll(groups, (-offset) % 8, 1)
        total = weight * moved if total is None else total + weight * moved
    return total.reshape(rows, features)


def winds(line):
    pair = line[:, 128:]
    swapped = pltpu.roll(pair, LEV, 1)
    first = iota(pair.shape, 1) < LEV
    return jnp.where(first, pair, swapped), jnp.where(first, swapped, pair)


def advect(line, along_x, along_y):
    u, v = winds(line)
    return jnp.concatenate(
        [
            -(u * along_x[:, :128] + v * along_y[:, :128]),
            -(u * along_x[:, 128:] + v * along_y[:, 128:]),
        ],
        axis=1,
    )


def across(lines, i):
    total = TABLE[i][0] * lines[0]
    for j in range(1, 4):
        total = total + TABLE[i][j] * lines[j]
    return total


def smooth_rows(line):
    rows, features = line.shape
    row = iota((rows, features), 0)
    phase = row % 4
    before = jnp.where(row == 0, 0.0, pltpu.roll(line, 1, 0))
    after = jnp.where(row == rows - 1, 0.0, pltpu.roll(line, rows - 1, 0))
    return jnp.where(
        phase == 0,
        0.5 * (line + before),
        jnp.where(phase == 3, 0.5 * (line + after), line),
    )


def edges_kernel(state, x_low, x_high, y_low, y_high):
    size_x, size_y, _ = state.shape
    for out, base, i in ((x_low, 0, 0), (x_high, size_x - 4, 3)):
        lines = [state[base + j] for j in range(4)]
        out[...] = advect(lines[i], across(lines, i), along_rows(lines[i]))
    for out, base, i in ((y_low, 0, 0), (y_high, size_y - 4, 3)):
        lines = [state[:, base + j, :] for j in range(4)]
        out[...] = advect(lines[i], along_rows(lines[i]), across(lines, i))


def sides_kernel(y_low, y_high, x_before, x_after, partial, slot_row, low, high):
    size, features = y_low.shape
    row = iota((size, features), 0)
    for out, line, y in ((low, y_low, 0), (high, y_high, size - 1)):
        extra = jnp.where(
            row == 0,
            0.5 * x_before[y : y + 1, :],
            jnp.where(row == size - 1, 0.5 * x_after[y : y + 1, :], 0.0),
        )
        out[...] = smooth_rows(line[...]) + extra


def local_kernel(state, token, partial, tend):
    size_x, size_y, features = state.shape
    tend[0] = jnp.zeros((size_y, features), F32)
    tend[size_x + 1] = jnp.zeros((size_y, features), F32)

    @pl.loop(0, size_x // 4)
    def _(e):
        lines = [state[4 * e + j] for j in range(4)]
        for i in range(4):
            tend[4 * e + i + 1] = advect(lines[i], across(lines, i), along_rows(lines[i]))

    @pl.loop(0, size_x // 4)
    def _(e):
        low = 4 * e + 1
        values = [
            0.5 * (tend[low] + tend[low - 1]),
            tend[low + 1],
            tend[low + 2],
            0.5 * (tend[low + 3] + tend[low + 4]),
        ]
        for i in range(4):
            partial[4 * e + i] = state[4 * e + i] + STEP_DT * smooth_rows(values[i])


def dot_parts(hot, values):
    total = None
    for _ in range(3):
        part = values.astype(BF16)
        term = dot(hot, part)
        total = term if total is None else total + term
        values = values - part.astype(F32)
    return total


def owner_ranks(owners):
    count = owners.shape[1]
    earlier = (iota((count, count), 0) < iota((count, count), 1)).astype(F32).astype(BF16)
    hot = (iota((128, count), 0) == owners).astype(F32)
    rank = jnp.sum(dot(hot.astype(BF16), earlier) * hot, axis=0, keepdims=True)
    return hot, rank.astype(jnp.int32)


def position(device, sizes):
    size_gx, size_gy = sizes
    return device % size_gy * size_gx + device // size_gy


def route_kernel(sizes, capacity, size_y, member_row, slot_row, hot_rows, hot_sides):
    columns = member_row.shape[1]
    size_x = columns // size_y
    earlier = (iota((128, 128), 0) < iota((128, 128), 1)).astype(F32).astype(BF16)
    seen = jnp.zeros((128, 1), F32)
    for b in range(columns // 128):
        part = slice(b * 128, (b + 1) * 128)
        members = position(member_row[:, part], sizes)
        hot = (iota((128, 128), 0) == members).astype(F32)
        count = dot(hot.astype(BF16), earlier) + seen
        rank = jnp.sum(count * hot, axis=0, keepdims=True).astype(jnp.int32)
        slot_row[:, part] = members * capacity + rank
        seen = seen + jnp.sum(hot, axis=1, keepdims=True)
    step = 256
    slots = slot_row[...]
    for b in range(hot_rows.shape[0] // step):
        hot = iota((step, columns), 0) + b * step == slots
        hot_rows[b * step : (b + 1) * step, :] = hot.astype(F32).astype(BF16)
    lane = iota((columns, 128), 1)
    place = (lane % size_x) * size_y + (lane // size_x) * (size_y - 1)
    choose = ((iota((columns, 128), 0) == place) & (lane < 2 * size_x)).astype(F32).astype(BF16)
    row = iota((8, columns), 0)
    both = jnp.where(row == 0, slots // capacity, jnp.where(row == 1, slots % capacity, 0))
    both = dot(both.astype(F32).astype(BF16), choose).astype(jnp.int32)
    side = both[0:1, :] * capacity + both[1:2, :]
    side = jnp.where(iota((1, 128), 1) < 2 * size_x, side, -1)
    for b in range(hot_sides.shape[0] // step):
        hot = iota((step, 128), 0) + b * step == side
        hot_sides[b * step : (b + 1) * step, :] = hot.astype(F32).astype(BF16)


def add_before_after(advanced, partial, x_before, x_after):
    size_x, _, _ = partial.shape
    advanced[...] = partial[...]
    half = 0.5 * STEP_DT
    advanced[0] = advanced[0] + half * smooth_rows(x_before[...])
    advanced[size_x - 1] = advanced[size_x - 1] + half * smooth_rows(x_after[...])


def inner_kernel(partial, x_before, x_after, hot_rows, send, sides, advanced):
    size_x, size_y, features = partial.shape
    add_before_after(advanced, partial, x_before, x_after)
    for i, y in enumerate((0, size_y - 1)):
        sides[i * size_x : (i + 1) * size_x, :] = advanced[:, y, :]
        advanced[:, y, :] = jnp.zeros((size_x, features), F32)
    columns = advanced[...].reshape(size_x * size_y, features).astype(BF16)
    step = 256
    for b in range(send.shape[0] // step):
        part = slice(b * step, (b + 1) * step)
        send[part, :] = dot(hot_rows[part, :], columns).astype(BF16)


def pack_kernel(inner, sides, y_before, y_after, hot_sides, members, send):
    half = 0.5 * STEP_DT
    size, features = y_before.shape
    columns = jnp.concatenate(
        [
            sides[0:size, :] + half * y_before[...],
            sides[size : 2 * size, :] + half * y_after[...],
            jnp.zeros((128 - 2 * size, features), F32),
        ],
        axis=0,
    ).astype(BF16)
    step = 512
    for b in range(send.shape[0] // step):
        part = slice(b * step, (b + 1) * step)
        send[part, :] = inner[part, :] + dot(hot_sides[part, :], columns).astype(BF16)


def as_column(row):
    wide = jnp.where(iota((128, 128), 0) == iota((128, 128), 1), row, 0)
    return jnp.sum(wide, axis=1, keepdims=True)


def prepare_kernel(capacity, size_y, element_row, weight, slot_row, sides, members, ranks, tiled):
    count = element_row.shape[1]
    lane = iota((count, 128), 1)
    for c in range(8):
        part = weight[:, (c // 4) * 128 : (c // 4 + 1) * 128]
        low = jnp.where(lane // 16 == 2 * c % 8, part, 0.0)
        high = jnp.where(lane // 16 == 2 * c % 8 + 1, part, 0.0)
        for distance in (64, 32, 16):
            low = low + pltpu.roll(low, distance, 1)
            high = high + pltpu.roll(high, distance, 1)
        tiled[c] = jnp.where(lane < 64, low, high)

    columns = slot_row.shape[1]
    elements_y = size_y // 4
    table = []
    for b in range(columns // 128):
        slots = as_column(slot_row[:, b * 128 : (b + 1) * 128])
        column = iota((128, 128), 0) + b * 128
        here = column // size_y % 4 * 4 + column % 4 == lane
        member = jnp.where(here, slots // capacity, 0).astype(F32)
        rank = jnp.where(here, slots % capacity, 0).astype(F32)
        table.append(jnp.concatenate([member, rank], axis=1).astype(BF16))
    column = iota((128, columns), 1)
    element = column // (4 * size_y) * elements_y + column % size_y // 4
    hot = (iota((128, columns), 0) == element).astype(F32).astype(BF16)
    by_element = dot(hot, jnp.concatenate(table, axis=0)).astype(BF16)
    hot = (lane == as_column(element_row[...])).astype(F32).astype(BF16)
    both = dot(hot, by_element)
    members[...] = both[:, :128].astype(jnp.int32)
    ranks[...] = both[:, 128:].astype(jnp.int32)


def silu_of_half(half):
    return half + half * jnp.tanh(half)


def first_kernel(sizes, rows, w_in, b_in, owner_row, block_row, out, blocks, w_half):
    owners = position(owner_row[...], sizes)
    hot, rank = owner_ranks(owners)
    values = block_row[...].astype(F32)
    lane = iota(blocks.shape, 1)
    first = jnp.sum(jnp.where(rank == 0, hot, 0.0) * values, axis=1, keepdims=True)
    second = jnp.sum(jnp.where(rank == 1, hot, 0.0) * values, axis=1, keepdims=True)
    blocks[...] = jnp.where(lane == 0, first, jnp.where(lane == 1, second, 0.0))

    w_half[...] = w_in[0] * jnp.asarray(0.5, BF16)
    b_half = 0.5 * b_in[...]
    step = 512
    for b in range(rows.shape[0] // step):
        part = slice(b * step, (b + 1) * step)
        out[part, :] = silu_of_half(dot(rows[part, :], w_half[...]) + b_half).astype(BF16)


def message_parts():
    return [((4 * h + q) * 128, 4 * q, 128 * h) for h in range(2) for q in range(4)]


def dot_by_output(a, b):
    return lax.dot_general(a, b, (((1,), (1,)), ((), ())), preferred_element_type=F32)


def second_kernel(first, w_mid, b_mid, w_last, blocks, out, w_half, w_flux):
    step = 512
    sources = step // 16
    lane = iota((step, 128), 1)
    own = lane // 8 == iota((step, 128), 0) % 16
    line = iota((sources, 4, 128), 1)
    w_half[...] = w_mid[0] * jnp.asarray(0.5, BF16)
    w_flux[...] = jnp.concatenate([w_last[0, 256:264, :].astype(F32)] * 16).astype(BF16)
    b_half = 0.5 * b_mid[...]
    for b in range(first.shape[0] // step):
        hidden = dot(first[b * step : (b + 1) * step, :], w_half[...])
        hidden = silu_of_half(hidden + b_half).astype(BF16)
        tends = dot_by_output(hidden, w_last[0, 0:256, :]).reshape(sources, 16, 256)
        part = slice(b * sources, (b + 1) * sources)
        for place, slot, feature in message_parts():
            out[part, :, place : place + 128] = tends[
                :, slot : slot + 4, feature : feature + 128
            ].astype(BF16)
        flux = jnp.where(own, dot_by_output(hidden, w_flux[...]), 0.0)
        flux = jnp.sum(flux.reshape(sources, 16, 128), axis=1, keepdims=True)
        names = blocks[part, :].reshape(sources, 1, 128)
        tail = jnp.where(line == 0, flux, jnp.where(line == 1, names, 0.0))
        out[part, :, 1024:1152] = tail.astype(BF16)


def contribution_kernel(sizes, answer, members, ranks, tiled, owner_row, send):
    flux = answer[:, :, 1024:1152].astype(F32)[:, 0, :].astype(BF16)
    spread = (iota((128, 128), 0) % 8 == iota((128, 128), 1) // 16).astype(F32).astype(BF16)
    lane = iota((128, 128), 1)
    group = lane // 8
    owners = position(owner_row[...], sizes)
    _, rank = owner_ranks(owners)
    hot = (iota(send.shape, 0) == owners * 2 + rank).astype(F32).astype(BF16)
    total = None
    for c in range(16):
        if c % 2 == 0:
            pair = tiled[c // 2]
            swapped = pltpu.roll(pair, 64, 1)
        weights = jnp.where(lane < 64, *((pair, swapped) if c % 2 == 0 else (swapped, pair)))
        pick = (lane == members[:, c : c + 1]).astype(F32).astype(BF16)
        value = jnp.where(group == ranks[:, c : c + 1], dot(pick, flux), 0.0)
        term = dot(value.astype(BF16), spread) * weights
        total = term if total is None else total + term
    send[...] = dot_parts(hot, total)


def columns_kernel(
    answer,
    slot_row,
    partial,
    x_before,
    x_after,
    y_before,
    y_after,
    new_state,
    sums,
    rows,
    wide,
    advanced,
):
    sources = answer.shape[0]
    slots = sources * 16
    size_x, size_y, features = partial.shape
    add_before_after(advanced, partial, x_before, x_after)
    half = 0.5 * STEP_DT
    advanced[:, 0, :] = advanced[:, 0, :] + half * y_before[...]
    advanced[:, size_y - 1, :] = advanced[:, size_y - 1, :] + half * y_after[...]
    for place, slot, feature in message_parts():
        wide[:, slot : slot + 4, feature : feature + 128] = answer[
            :, :, place : place + 128
        ].astype(F32)
    rows[...] = wide[...].reshape(slots, features).astype(BF16)
    step = 128
    lines = step // size_y
    for b in range(size_x // lines):
        hot = iota((step, slots), 1) == as_column(slot_row[:, b * step : (b + 1) * step])
        tends = dot(hot.astype(F32).astype(BF16), rows[...])
        part = slice(b * lines, (b + 1) * lines)
        new_state[part] = advanced[part] + tends.reshape(lines, size_y, features)
    names = answer[:, :, 1024:1152].astype(F32)[:, 1, :]
    lane = iota((sources, 128), 1)
    for j in range(2):
        hot = (names[:, j : j + 1].astype(jnp.int32) == lane).astype(F32)
        sums[j] = jnp.transpose(hot)[:OB_DEV, :]


def ocean_kernel(received, sums, out):
    out[...] = dot(sums[0], received[:, 0, :], HIGHEST) + dot(sums[1], received[:, 1, :], HIGHEST)


def call(kernel, outs, *args, flops=0, nbytes=0, transcendentals=0, scratch=(), limit=16, spaces=None, out_spaces=None):
    return pl.pallas_call(
        kernel,
        out_shape=[jax.ShapeDtypeStruct(s, d) for s, d in outs],
        in_specs=[
            pl.BlockSpec(memory_space=(spaces or {}).get(i, pltpu.VMEM)) for i in range(len(args))
        ],
        out_specs=[
            pl.BlockSpec(memory_space=(out_spaces or {}).get(i, pltpu.VMEM))
            for i in range(len(outs))
        ],
        scratch_shapes=list(scratch),
        compiler_params=pltpu.CompilerParams(vmem_limit_bytes=limit * MIB),
        cost_estimate=pl.CostEstimate(
            flops=flops, bytes_accessed=nbytes, transcendentals=transcendentals
        ),
    )(*args)


def shift(value, axis, step):
    size = lax.axis_size(axis)
    return lax.ppermute(value, axis, [(i, (i + step) % size) for i in range(size)])


def exchange(value):
    return lax.all_to_all(value, AXES, split_axis=0, concat_axis=0, tiled=True)


def shards(
    state,
    group_member,
    w_in,
    bias_in,
    w_mid,
    bias_mid,
    w_out,
    intersection_element,
    ocean_owner,
    ocean_block,
    regrid_weight,
):
    size_x, size_y, features = state.shape
    sizes = lax.axis_size("gx"), lax.axis_size("gy")
    devices = sizes[0] * sizes[1]
    columns = size_x * size_y
    capacity = 2 * columns // devices
    slots = devices * capacity
    count = intersection_element.shape[0]
    line = ((size_x, features), F32)

    x_low, x_high, y_low, y_high = call(
        edges_kernel,
        [line] * 4,
        state,
        nbytes=2 * MIB,
        flops=MIB,
    )
    x_before, x_after = shift(x_high, "gx", 1), shift(x_low, "gx", -1)

    def local(token):
        return call(
            local_kernel,
            [(state.shape, F32)],
            state,
            token,
            nbytes=8 * MIB,
            flops=64 * MIB,
            spaces={1: pl.ANY},
            scratch=[pltpu.VMEM((size_x + 2, size_y, features), F32)],
        )[0]

    partial = local(x_low)
    slot_row, hot_rows, hot_sides = call(
        lambda *refs: route_kernel(sizes, capacity, size_y, *refs),
        [((1, columns), jnp.int32), ((slots, columns), BF16), ((slots, 128), BF16)],
        group_member.reshape(1, columns),
        nbytes=8 * MIB,
        flops=64 * MIB,
    )
    low, high = call(
        sides_kernel,
        [line] * 2,
        y_low,
        y_high,
        x_before,
        x_after,
        partial,
        slot_row,
        spaces={4: pl.ANY, 5: pl.ANY},
    )
    y_before, y_after = shift(high, "gy", 1), shift(low, "gy", -1)
    inner, sides = call(
        inner_kernel,
        [((slots, features), BF16), ((2 * size_x, features), F32)],
        partial,
        x_before,
        x_after,
        hot_rows,
        nbytes=8 * MIB,
        flops=2 * slots * columns * features,
        scratch=[pltpu.VMEM(state.shape, F32)],
    )
    members, ranks, tiled = call(
        lambda *refs: prepare_kernel(capacity, size_y, *refs),
        [((count, 128), jnp.int32)] * 2 + [((8, count, 128), F32)],
        intersection_element.reshape(1, count),
        regrid_weight,
        slot_row,
        sides,
        spaces={3: pl.ANY},
        nbytes=12 * MIB,
        flops=2 * 16 * count * columns * 256,
    )
    (send,) = call(
        pack_kernel,
        [((slots, features), BF16)],
        inner,
        sides,
        y_before,
        y_after,
        hot_sides,
        members,
        nbytes=4 * MIB,
        flops=2 * slots * 128 * features,
        spaces={5: pl.ANY},
    )
    received = exchange(send.reshape(devices, capacity, features)).reshape(slots, features)

    hidden = w_in.shape[2]
    owner_row = ocean_owner.reshape(1, count)
    first, blocks = call(
        lambda *refs: first_kernel(sizes, *refs),
        [((slots, hidden), BF16), ((devices, 128), F32)],
        received,
        w_in,
        bias_in,
        owner_row,
        ocean_block.reshape(1, count),
        nbytes=6 * MIB,
        flops=2 * slots * features * hidden,
        transcendentals=slots * hidden,
        scratch=[pltpu.VMEM((features, hidden), BF16)],
    )
    (answered,) = call(
        second_kernel,
        [((devices, 4, 1152), BF16)],
        first,
        w_mid,
        bias_mid,
        jnp.swapaxes(w_out, 1, 2),
        blocks,
        nbytes=8 * MIB,
        flops=2 * slots * hidden * (hidden + 384),
        transcendentals=slots * hidden,
        limit=24,
        scratch=[pltpu.VMEM((hidden, hidden), BF16), pltpu.VMEM((128, hidden), BF16)],
    )
    answer = exchange(answered)
    (ocean_send,) = call(
        lambda *refs: contribution_kernel(sizes, *refs),
        [((2 * devices, 128), F32)],
        answer,
        members,
        ranks,
        tiled,
        owner_row,
        nbytes=4 * MIB,
        flops=2 * 2 * 2048 * 128 * 128,
    )
    ocean_got = exchange(ocean_send.reshape(devices, 2, 128))
    partial = local(ocean_send)
    new_state, sums = call(
        columns_kernel,
        [(state.shape, F32), ((2, OB_DEV, devices), F32)],
        answer,
        slot_row,
        partial,
        x_before,
        x_after,
        y_before,
        y_after,
        nbytes=12 * MIB,
        flops=2 * slots * columns * features,
        scratch=[
            pltpu.VMEM((slots, features), BF16),
            pltpu.VMEM((devices, 16, features), F32),
            pltpu.VMEM(state.shape, F32),
        ],
    )
    (ocean_total,) = call(
        ocean_kernel, [((OB_DEV, 128), F32)], ocean_got, sums, nbytes=MIB, flops=MIB
    )
    return (new_state, ocean_total)


def solution(mesh):
    return jax.shard_map(
        shards,
        mesh=mesh,
        in_specs=(
            P("gx", "gy", None),
            P(("gx", "gy"), None),
            P(("gx", "gy"), None, None),
            P(("gx", "gy"), None),
            P(("gx", "gy"), None, None),
            P(("gx", "gy"), None),
            P(("gx", "gy"), None, None),
            P(("gx", "gy")),
            P(("gx", "gy"), None),
            P(("gx", "gy")),
            P(("gx", "gy"), None),
        ),
        out_specs=(P("gx", "gy", None), P(("gx", "gy"), None)),
        check_vma=False,
    )
```

```python
import math

import jax
import jax.numpy as jnp
import numpy as np
from jax import lax
from jax.experimental import pallas as pl
from jax.experimental.pallas import tpu as pltpu
from jax.sharding import PartitionSpec as P

LEV = 64
OB_DEV = 16
STEP_DT = 0.2
HIGHEST = lax.Precision.HIGHEST
AXES = ("gy", "gx")
F32 = jnp.float32
BF16 = jnp.bfloat16
MIB = 1 << 20


def derivative_table():
    root = 1.0 / math.sqrt(5.0)
    nodes = np.array([-1.0, -root, root, 1.0])
    table = np.zeros((4, 4))
    for row_index in range(4):
        for col_index in range(4):
            if row_index == col_index:
                table[row_index, col_index] = sum(
                    (
                        1.0 / (nodes[row_index] - nodes[other])
                        for other in range(4)
                        if other != row_index
                    )
                )
            else:
                weight_row = np.prod(
                    [nodes[row_index] - nodes[other] for other in range(4) if other != row_index]
                )
                weight_col = np.prod(
                    [nodes[col_index] - nodes[other] for other in range(4) if other != col_index]
                )
                table[row_index, col_index] = weight_row / (
                    weight_col * (nodes[row_index] - nodes[col_index])
                )
    return table


TABLE = [[float(np.float32(v)) for v in row] for row in derivative_table()]


def iota(shape, dim):
    return lax.broadcasted_iota(jnp.int32, shape, dim)


def dot(a, b, precision=None):
    return jnp.dot(a, b, preferred_element_type=F32, precision=precision)


def along_rows(line):
    rows, features = line.shape
    groups = line.reshape(rows // 8, 8, features)
    phase = iota((1, 8, features), 1) % 4
    total = None
    for offset in range(-3, 4):
        weight = jnp.zeros((1, 8, features), F32)
        for p in range(4):
            if 0 <= p + offset < 4:
                weight = jnp.where(phase == p, TABLE[p][p + offset], weight)
        moved = groups if offset == 0 else pltpu.roll(groups, (-offset) % 8, 1)
        total = weight * moved if total is None else total + weight * moved
    return total.reshape(rows, features)


def winds(line):
    pair = line[:, 128:]
    swapped = pltpu.roll(pair, LEV, 1)
    first = iota(pair.shape, 1) < LEV
    return jnp.where(first, pair, swapped), jnp.where(first, swapped, pair)


def advect(line, along_x, along_y):
    u, v = winds(line)
    return jnp.concatenate(
        [
            -(u * along_x[:, :128] + v * along_y[:, :128]),
            -(u * along_x[:, 128:] + v * along_y[:, 128:]),
        ],
        axis=1,
    )


def across(lines, i):
    total = TABLE[i][0] * lines[0]
    for j in range(1, 4):
        total = total + TABLE[i][j] * lines[j]
    return total


def smooth_rows(line):
    rows, features = line.shape
    row = iota((rows, features), 0)
    phase = row % 4
    before = jnp.where(row == 0, 0.0, pltpu.roll(line, 1, 0))
    after = jnp.where(row == rows - 1, 0.0, pltpu.roll(line, rows - 1, 0))
    return jnp.where(
        phase == 0,
        0.5 * (line + before),
        jnp.where(phase == 3, 0.5 * (line + after), line),
    )


def edges_kernel(state, x_low, x_high, y_low, y_high):
    size_x, size_y, _ = state.shape
    for out, base, i in ((x_low, 0, 0), (x_high, size_x - 4, 3)):
        lines = [state[base + j] for j in range(4)]
        out[...] = advect(lines[i], across(lines, i), along_rows(lines[i]))
    for out, base, i in ((y_low, 0, 0), (y_high, size_y - 4, 3)):
        lines = [state[:, base + j, :] for j in range(4)]
        out[...] = advect(lines[i], along_rows(lines[i]), across(lines, i))


def sides_kernel(y_low, y_high, x_before, x_after, partial, slot_row, low, high):
    size, features = y_low.shape
    row = iota((size, features), 0)
    for out, line, y in ((low, y_low, 0), (high, y_high, size - 1)):
        extra = jnp.where(
            row == 0,
            0.5 * x_before[y : y + 1, :],
            jnp.where(row == size - 1, 0.5 * x_after[y : y + 1, :], 0.0),
        )
        out[...] = smooth_rows(line[...]) + extra


def local_kernel(state, token, partial, tend):
    size_x, size_y, features = state.shape
    tend[0] = jnp.zeros((size_y, features), F32)
    tend[size_x + 1] = jnp.zeros((size_y, features), F32)

    @pl.loop(0, size_x // 4)
    def _(e):
        lines = [state[4 * e + j] for j in range(4)]
        for i in range(4):
            tend[4 * e + i + 1] = advect(lines[i], across(lines, i), along_rows(lines[i]))

    @pl.loop(0, size_x // 4)
    def _(e):
        low = 4 * e + 1
        values = [
            0.5 * (tend[low] + tend[low - 1]),
            tend[low + 1],
            tend[low + 2],
            0.5 * (tend[low + 3] + tend[low + 4]),
        ]
        for i in range(4):
            partial[4 * e + i] = state[4 * e + i] + STEP_DT * smooth_rows(values[i])


def dot_parts(hot, values):
    total = None
    for _ in range(3):
        part = values.astype(BF16)
        term = dot(hot, part)
        total = term if total is None else total + term
        values = values - part.astype(F32)
    return total


def owner_ranks(owners):
    count = owners.shape[1]
    earlier = (iota((count, count), 0) < iota((count, count), 1)).astype(F32).astype(BF16)
    hot = (iota((128, count), 0) == owners).astype(F32)
    rank = jnp.sum(dot(hot.astype(BF16), earlier) * hot, axis=0, keepdims=True)
    return hot, rank.astype(jnp.int32)


def position(device, sizes):
    size_gx, size_gy = sizes
    return device % size_gy * size_gx + device // size_gy


def route_kernel(sizes, capacity, size_y, member_row, slot_row, hot_rows, hot_sides):
    columns = member_row.shape[1]
    size_x = columns // size_y
    earlier = (iota((128, 128), 0) < iota((128, 128), 1)).astype(F32).astype(BF16)
    seen = jnp.zeros((128, 1), F32)
    for b in range(columns // 128):
        part = slice(b * 128, (b + 1) * 128)
        members = position(member_row[:, part], sizes)
        hot = (iota((128, 128), 0) == members).astype(F32)
        count = dot(hot.astype(BF16), earlier) + seen
        rank = jnp.sum(count * hot, axis=0, keepdims=True).astype(jnp.int32)
        slot_row[:, part] = members * capacity + rank
        seen = seen + jnp.sum(hot, axis=1, keepdims=True)
    step = 256
    slots = slot_row[...]
    for b in range(hot_rows.shape[0] // step):
        hot = iota((step, columns), 0) + b * step == slots
        hot_rows[b * step : (b + 1) * step, :] = hot.astype(F32).astype(BF16)
    lane = iota((columns, 128), 1)
    place = (lane % size_x) * size_y + (lane // size_x) * (size_y - 1)
    choose = ((iota((columns, 128), 0) == place) & (lane < 2 * size_x)).astype(F32).astype(BF16)
    row = iota((8, columns), 0)
    both = jnp.where(row == 0, slots // capacity, jnp.where(row == 1, slots % capacity, 0))
    both = dot(both.astype(F32).astype(BF16), choose).astype(jnp.int32)
    side = both[0:1, :] * capacity + both[1:2, :]
    side = jnp.where(iota((1, 128), 1) < 2 * size_x, side, -1)
    for b in range(hot_sides.shape[0] // step):
        hot = iota((step, 128), 0) + b * step == side
        hot_sides[b * step : (b + 1) * step, :] = hot.astype(F32).astype(BF16)


def add_before_after(advanced, partial, x_before, x_after):
    size_x, _, _ = partial.shape
    advanced[...] = partial[...]
    half = 0.5 * STEP_DT
    advanced[0] = advanced[0] + half * smooth_rows(x_before[...])
    advanced[size_x - 1] = advanced[size_x - 1] + half * smooth_rows(x_after[...])


def inner_kernel(partial, x_before, x_after, hot_rows, send, sides, advanced):
    size_x, size_y, features = partial.shape
    add_before_after(advanced, partial, x_before, x_after)
    for i, y in enumerate((0, size_y - 1)):
        sides[i * size_x : (i + 1) * size_x, :] = advanced[:, y, :]
        advanced[:, y, :] = jnp.zeros((size_x, features), F32)
    columns = advanced[...].reshape(size_x * size_y, features).astype(BF16)
    step = 256
    for b in range(send.shape[0] // step):
        part = slice(b * step, (b + 1) * step)
        send[part, :] = dot(hot_rows[part, :], columns).astype(BF16)


def pack_kernel(inner, sides, y_before, y_after, hot_sides, members, send):
    half = 0.5 * STEP_DT
    size, features = y_before.shape
    columns = jnp.concatenate(
        [
            sides[0:size, :] + half * y_before[...],
            sides[size : 2 * size, :] + half * y_after[...],
            jnp.zeros((128 - 2 * size, features), F32),
        ],
        axis=0,
    ).astype(BF16)
    step = 512
    for b in range(send.shape[0] // step):
        part = slice(b * step, (b + 1) * step)
        send[part, :] = inner[part, :] + dot(hot_sides[part, :], columns).astype(BF16)


def as_column(row):
    wide = jnp.where(iota((128, 128), 0) == iota((128, 128), 1), row, 0)
    return jnp.sum(wide, axis=1, keepdims=True)


def prepare_kernel(capacity, size_y, element_row, weight, slot_row, sides, members, ranks, tiled):
    count = element_row.shape[1]
    lane = iota((count, 128), 1)
    for c in range(8):
        part = weight[:, (c // 4) * 128 : (c // 4 + 1) * 128]
        low = jnp.where(lane // 16 == 2 * c % 8, part, 0.0)
        high = jnp.where(lane // 16 == 2 * c % 8 + 1, part, 0.0)
        for distance in (64, 32, 16):
            low = low + pltpu.roll(low, distance, 1)
            high = high + pltpu.roll(high, distance, 1)
        tiled[c] = jnp.where(lane < 64, low, high)

    columns = slot_row.shape[1]
    elements_y = size_y // 4
    table = []
    for b in range(columns // 128):
        slots = as_column(slot_row[:, b * 128 : (b + 1) * 128])
        column = iota((128, 128), 0) + b * 128
        here = column // size_y % 4 * 4 + column % 4 == lane
        member = jnp.where(here, slots // capacity, 0).astype(F32)
        rank = jnp.where(here, slots % capacity, 0).astype(F32)
        table.append(jnp.concatenate([member, rank], axis=1).astype(BF16))
    column = iota((128, columns), 1)
    element = column // (4 * size_y) * elements_y + column % size_y // 4
    hot = (iota((128, columns), 0) == element).astype(F32).astype(BF16)
    by_element = dot(hot, jnp.concatenate(table, axis=0)).astype(BF16)
    hot = (lane == as_column(element_row[...])).astype(F32).astype(BF16)
    both = dot(hot, by_element)
    members[...] = both[:, :128].astype(jnp.int32)
    ranks[...] = both[:, 128:].astype(jnp.int32)


def silu_of_half(half):
    return half + half * jnp.tanh(half)


def first_kernel(sizes, rows, w_in, b_in, owner_row, block_row, out, blocks, w_half):
    owners = position(owner_row[...], sizes)
    hot, rank = owner_ranks(owners)
    values = block_row[...].astype(F32)
    lane = iota(blocks.shape, 1)
    first = jnp.sum(jnp.where(rank == 0, hot, 0.0) * values, axis=1, keepdims=True)
    second = jnp.sum(jnp.where(rank == 1, hot, 0.0) * values, axis=1, keepdims=True)
    blocks[...] = jnp.where(lane == 0, first, jnp.where(lane == 1, second, 0.0))

    w_half[...] = w_in[0] * jnp.asarray(0.5, BF16)
    b_half = 0.5 * b_in[...]
    step = 512
    for b in range(rows.shape[0] // step):
        part = slice(b * step, (b + 1) * step)
        out[part, :] = silu_of_half(dot(rows[part, :], w_half[...]) + b_half).astype(BF16)


def message_parts():
    return [((8 * h + q) * 128, 2 * q, 128 * h) for h in range(2) for q in range(8)]


def dot_by_output(a, b):
    return lax.dot_general(a, b, (((1,), (1,)), ((), ())), preferred_element_type=F32)


def second_kernel(first, w_mid, b_mid, w_last, blocks, out, w_half, w_flux):
    step = 512
    sources = step // 16
    lane = iota((step, 128), 1)
    own = lane // 8 == iota((step, 128), 0) % 16
    line = iota((sources, 2, 128), 1)
    w_half[...] = w_mid[0] * jnp.asarray(0.5, BF16)
    w_flux[...] = jnp.concatenate([w_last[0, 256:264, :].astype(F32)] * 16).astype(BF16)
    b_half = 0.5 * b_mid[...]
    for b in range(first.shape[0] // step):
        hidden = dot(first[b * step : (b + 1) * step, :], w_half[...])
        hidden = silu_of_half(hidden + b_half).astype(BF16)
        tends = dot_by_output(hidden, w_last[0, 0:256, :]).reshape(sources, 16, 256)
        part = slice(b * sources, (b + 1) * sources)
        for place, slot, feature in message_parts():
            out[part, :, place : place + 128] = tends[
                :, slot : slot + 2, feature : feature + 128
            ].astype(BF16)
        flux = jnp.where(own, dot_by_output(hidden, w_flux[...]), 0.0)
        flux = jnp.sum(flux.reshape(sources, 16, 128), axis=1, keepdims=True)
        names = blocks[part, :].reshape(sources, 1, 128)
        tail = jnp.where(line == 0, flux, jnp.where(line == 1, names, 0.0))
        out[part, :, 2048:2176] = tail.astype(BF16)


def contribution_kernel(sizes, answer, members, ranks, tiled, owner_row, send):
    flux = answer[:, :, 2048:2176].astype(F32)[:, 0, :].astype(BF16)
    spread = (iota((128, 128), 0) % 8 == iota((128, 128), 1) // 16).astype(F32).astype(BF16)
    lane = iota((128, 128), 1)
    group = lane // 8
    owners = position(owner_row[...], sizes)
    _, rank = owner_ranks(owners)
    hot = (iota(send.shape, 0) == owners * 2 + rank).astype(F32).astype(BF16)
    total = None
    for c in range(16):
        if c % 2 == 0:
            pair = tiled[c // 2]
            swapped = pltpu.roll(pair, 64, 1)
        weights = jnp.where(lane < 64, *((pair, swapped) if c % 2 == 0 else (swapped, pair)))
        pick = (lane == members[:, c : c + 1]).astype(F32).astype(BF16)
        value = jnp.where(group == ranks[:, c : c + 1], dot(pick, flux), 0.0)
        term = dot(value.astype(BF16), spread) * weights
        total = term if total is None else total + term
    send[...] = dot_parts(hot, total)


def columns_kernel(
    answer,
    slot_row,
    partial,
    x_before,
    x_after,
    y_before,
    y_after,
    new_state,
    sums,
    rows,
    wide,
    advanced,
):
    sources = answer.shape[0]
    slots = sources * 16
    size_x, size_y, features = partial.shape
    add_before_after(advanced, partial, x_before, x_after)
    half = 0.5 * STEP_DT
    advanced[:, 0, :] = advanced[:, 0, :] + half * y_before[...]
    advanced[:, size_y - 1, :] = advanced[:, size_y - 1, :] + half * y_after[...]
    for place, slot, feature in message_parts():
        wide[:, slot : slot + 2, feature : feature + 128] = answer[
            :, :, place : place + 128
        ].astype(F32)
    rows[...] = wide[...].reshape(slots, features).astype(BF16)
    step = 128
    lines = step // size_y
    for b in range(size_x // lines):
        hot = iota((step, slots), 1) == as_column(slot_row[:, b * step : (b + 1) * step])
        tends = dot(hot.astype(F32).astype(BF16), rows[...])
        part = slice(b * lines, (b + 1) * lines)
        new_state[part] = advanced[part] + tends.reshape(lines, size_y, features)
    names = answer[:, :, 2048:2176].astype(F32)[:, 1, :]
    lane = iota((sources, 128), 1)
    for j in range(2):
        hot = (names[:, j : j + 1].astype(jnp.int32) == lane).astype(F32)
        sums[j] = jnp.transpose(hot)[:OB_DEV, :]


def ocean_kernel(received, sums, out):
    out[...] = dot(sums[0], received[:, 0, :], HIGHEST) + dot(sums[1], received[:, 1, :], HIGHEST)


def call(kernel, outs, *args, flops=0, nbytes=0, transcendentals=0, scratch=(), limit=16, spaces=None, out_spaces=None):
    return pl.pallas_call(
        kernel,
        out_shape=[jax.ShapeDtypeStruct(s, d) for s, d in outs],
        in_specs=[
            pl.BlockSpec(memory_space=(spaces or {}).get(i, pltpu.VMEM)) for i in range(len(args))
        ],
        out_specs=[
            pl.BlockSpec(memory_space=(out_spaces or {}).get(i, pltpu.VMEM))
            for i in range(len(outs))
        ],
        scratch_shapes=list(scratch),
        compiler_params=pltpu.CompilerParams(vmem_limit_bytes=limit * MIB),
        cost_estimate=pl.CostEstimate(
            flops=flops, bytes_accessed=nbytes, transcendentals=transcendentals
        ),
    )(*args)


def shift(value, axis, step):
    size = lax.axis_size(axis)
    return lax.ppermute(value, axis, [(i, (i + step) % size) for i in range(size)])


def exchange(value):
    return lax.all_to_all(value, AXES, split_axis=0, concat_axis=0, tiled=True)


def shards(
    state,
    group_member,
    w_in,
    bias_in,
    w_mid,
    bias_mid,
    w_out,
    intersection_element,
    ocean_owner,
    ocean_block,
    regrid_weight,
):
    size_x, size_y, features = state.shape
    sizes = lax.axis_size("gx"), lax.axis_size("gy")
    devices = sizes[0] * sizes[1]
    columns = size_x * size_y
    capacity = 2 * columns // devices
    slots = devices * capacity
    count = intersection_element.shape[0]
    line = ((size_x, features), F32)

    x_low, x_high, y_low, y_high = call(
        edges_kernel,
        [line] * 4,
        state,
        nbytes=2 * MIB,
        flops=MIB,
    )
    x_before, x_after = shift(x_high, "gx", 1), shift(x_low, "gx", -1)

    def local(token):
        return call(
            local_kernel,
            [(state.shape, F32)],
            state,
            token,
            nbytes=8 * MIB,
            flops=64 * MIB,
            spaces={1: pl.ANY},
            scratch=[pltpu.VMEM((size_x + 2, size_y, features), F32)],
        )[0]

    partial = local(x_low)
    slot_row, hot_rows, hot_sides = call(
        lambda *refs: route_kernel(sizes, capacity, size_y, *refs),
        [((1, columns), jnp.int32), ((slots, columns), BF16), ((slots, 128), BF16)],
        group_member.reshape(1, columns),
        nbytes=8 * MIB,
        flops=64 * MIB,
    )
    low, high = call(
        sides_kernel,
        [line] * 2,
        y_low,
        y_high,
        x_before,
        x_after,
        partial,
        slot_row,
        spaces={4: pl.ANY, 5: pl.ANY},
    )
    y_before, y_after = shift(high, "gy", 1), shift(low, "gy", -1)
    inner, sides = call(
        inner_kernel,
        [((slots, features), BF16), ((2 * size_x, features), F32)],
        partial,
        x_before,
        x_after,
        hot_rows,
        nbytes=8 * MIB,
        flops=2 * slots * columns * features,
        scratch=[pltpu.VMEM(state.shape, F32)],
    )
    members, ranks, tiled = call(
        lambda *refs: prepare_kernel(capacity, size_y, *refs),
        [((count, 128), jnp.int32)] * 2 + [((8, count, 128), F32)],
        intersection_element.reshape(1, count),
        regrid_weight,
        slot_row,
        sides,
        spaces={3: pl.ANY},
        nbytes=12 * MIB,
        flops=2 * 16 * count * columns * 256,
    )
    (send,) = call(
        pack_kernel,
        [((slots, features), BF16)],
        inner,
        sides,
        y_before,
        y_after,
        hot_sides,
        members,
        nbytes=4 * MIB,
        flops=2 * slots * 128 * features,
        spaces={5: pl.ANY},
    )
    received = exchange(send.reshape(devices, capacity, features)).reshape(slots, features)

    hidden = w_in.shape[2]
    owner_row = ocean_owner.reshape(1, count)
    first, blocks = call(
        lambda *refs: first_kernel(sizes, *refs),
        [((slots, hidden), BF16), ((devices, 128), F32)],
        received,
        w_in,
        bias_in,
        owner_row,
        ocean_block.reshape(1, count),
        nbytes=6 * MIB,
        flops=2 * slots * features * hidden,
        transcendentals=slots * hidden,
        scratch=[pltpu.VMEM((features, hidden), BF16)],
    )
    (answered,) = call(
        second_kernel,
        [((devices, 2, 2176), BF16)],
        first,
        w_mid,
        bias_mid,
        jnp.swapaxes(w_out, 1, 2),
        blocks,
        nbytes=8 * MIB,
        flops=2 * slots * hidden * (hidden + 384),
        transcendentals=slots * hidden,
        limit=24,
        scratch=[pltpu.VMEM((hidden, hidden), BF16), pltpu.VMEM((128, hidden), BF16)],
    )
    answer = exchange(answered)
    (ocean_send,) = call(
        lambda *refs: contribution_kernel(sizes, *refs),
        [((2 * devices, 128), F32)],
        answer,
        members,
        ranks,
        tiled,
        owner_row,
        nbytes=4 * MIB,
        flops=2 * 2 * 2048 * 128 * 128,
    )
    ocean_got = exchange(ocean_send.reshape(devices, 2, 128))
    partial = local(ocean_send)
    new_state, sums = call(
        columns_kernel,
        [(state.shape, F32), ((2, OB_DEV, devices), F32)],
        answer,
        slot_row,
        partial,
        x_before,
        x_after,
        y_before,
        y_after,
        nbytes=12 * MIB,
        flops=2 * slots * columns * features,
        scratch=[
            pltpu.VMEM((slots, features), BF16),
            pltpu.VMEM((devices, 16, features), F32),
            pltpu.VMEM(state.shape, F32),
        ],
    )
    (ocean_total,) = call(
        ocean_kernel, [((OB_DEV, 128), F32)], ocean_got, sums, nbytes=MIB, flops=MIB
    )
    return (new_state, ocean_total)


def solution(mesh):
    return jax.shard_map(
        shards,
        mesh=mesh,
        in_specs=(
            P("gx", "gy", None),
            P(("gx", "gy"), None),
            P(("gx", "gy"), None, None),
            P(("gx", "gy"), None),
            P(("gx", "gy"), None, None),
            P(("gx", "gy"), None),
            P(("gx", "gy"), None, None),
            P(("gx", "gy")),
            P(("gx", "gy"), None),
            P(("gx", "gy")),
            P(("gx", "gy"), None),
        ),
        out_specs=(P("gx", "gy", None), P(("gx", "gy"), None)),
        check_vma=False,
    )
```

```python
import math

import jax
import jax.numpy as jnp
import numpy as np
from jax import lax
from jax.experimental import pallas as pl
from jax.experimental.pallas import tpu as pltpu
from jax.sharding import PartitionSpec as P

LEV = 64
OB_DEV = 16
STEP_DT = 0.2
HIGHEST = lax.Precision.HIGHEST
AXES = ("gy", "gx")
F32 = jnp.float32
BF16 = jnp.bfloat16
MIB = 1 << 20


def derivative_table():
    root = 1.0 / math.sqrt(5.0)
    nodes = np.array([-1.0, -root, root, 1.0])
    table = np.zeros((4, 4))
    for row_index in range(4):
        for col_index in range(4):
            if row_index == col_index:
                table[row_index, col_index] = sum(
                    (
                        1.0 / (nodes[row_index] - nodes[other])
                        for other in range(4)
                        if other != row_index
                    )
                )
            else:
                weight_row = np.prod(
                    [nodes[row_index] - nodes[other] for other in range(4) if other != row_index]
                )
                weight_col = np.prod(
                    [nodes[col_index] - nodes[other] for other in range(4) if other != col_index]
                )
                table[row_index, col_index] = weight_row / (
                    weight_col * (nodes[row_index] - nodes[col_index])
                )
    return table


TABLE = [[float(np.float32(v)) for v in row] for row in derivative_table()]


def iota(shape, dim):
    return lax.broadcasted_iota(jnp.int32, shape, dim)


def dot(a, b, precision=None):
    return jnp.dot(a, b, preferred_element_type=F32, precision=precision)


def along_rows(line):
    rows, features = line.shape
    groups = line.reshape(rows // 8, 8, features)
    phase = iota((1, 8, features), 1) % 4
    total = None
    for offset in range(-3, 4):
        weight = jnp.zeros((1, 8, features), F32)
        for p in range(4):
            if 0 <= p + offset < 4:
                weight = jnp.where(phase == p, TABLE[p][p + offset], weight)
        moved = groups if offset == 0 else pltpu.roll(groups, (-offset) % 8, 1)
        total = weight * moved if total is None else total + weight * moved
    return total.reshape(rows, features)


def winds(line):
    pair = line[:, 128:]
    swapped = pltpu.roll(pair, LEV, 1)
    first = iota(pair.shape, 1) < LEV
    return jnp.where(first, pair, swapped), jnp.where(first, swapped, pair)


def advect(line, along_x, along_y):
    u, v = winds(line)
    return jnp.concatenate(
        [
            -(u * along_x[:, :128] + v * along_y[:, :128]),
            -(u * along_x[:, 128:] + v * along_y[:, 128:]),
        ],
        axis=1,
    )


def across(lines, i):
    total = TABLE[i][0] * lines[0]
    for j in range(1, 4):
        total = total + TABLE[i][j] * lines[j]
    return total


def smooth_rows(line):
    rows, features = line.shape
    row = iota((rows, features), 0)
    phase = row % 4
    before = jnp.where(row == 0, 0.0, pltpu.roll(line, 1, 0))
    after = jnp.where(row == rows - 1, 0.0, pltpu.roll(line, rows - 1, 0))
    return jnp.where(
        phase == 0,
        0.5 * (line + before),
        jnp.where(phase == 3, 0.5 * (line + after), line),
    )


def edges_kernel(state, x_low, x_high, y_low, y_high):
    size_x, size_y, _ = state.shape
    for out, base, i in ((x_low, 0, 0), (x_high, size_x - 4, 3)):
        lines = [state[base + j] for j in range(4)]
        out[...] = advect(lines[i], across(lines, i), along_rows(lines[i]))
    for out, base, i in ((y_low, 0, 0), (y_high, size_y - 4, 3)):
        lines = [state[:, base + j, :] for j in range(4)]
        out[...] = advect(lines[i], along_rows(lines[i]), across(lines, i))


def sides_kernel(y_low, y_high, x_before, x_after, partial, low, high):
    size, features = y_low.shape
    row = iota((size, features), 0)
    for out, line, y in ((low, y_low, 0), (high, y_high, size - 1)):
        extra = jnp.where(
            row == 0,
            0.5 * x_before[y : y + 1, :],
            jnp.where(row == size - 1, 0.5 * x_after[y : y + 1, :], 0.0),
        )
        out[...] = smooth_rows(line[...]) + extra


def local_kernel(state, token, partial, tend):
    size_x, size_y, features = state.shape
    tend[0] = jnp.zeros((size_y, features), F32)
    tend[size_x + 1] = jnp.zeros((size_y, features), F32)

    @pl.loop(0, size_x // 4)
    def _(e):
        lines = [state[4 * e + j] for j in range(4)]
        for i in range(4):
            tend[4 * e + i + 1] = advect(lines[i], across(lines, i), along_rows(lines[i]))

    @pl.loop(0, size_x // 4)
    def _(e):
        low = 4 * e + 1
        values = [
            0.5 * (tend[low] + tend[low - 1]),
            tend[low + 1],
            tend[low + 2],
            0.5 * (tend[low + 3] + tend[low + 4]),
        ]
        for i in range(4):
            partial[4 * e + i] = state[4 * e + i] + STEP_DT * smooth_rows(values[i])


def dot_parts(hot, values):
    total = None
    for _ in range(3):
        part = values.astype(BF16)
        term = dot(hot, part)
        total = term if total is None else total + term
        values = values - part.astype(F32)
    return total


def owner_ranks(owners):
    count = owners.shape[1]
    earlier = (iota((count, count), 0) < iota((count, count), 1)).astype(F32).astype(BF16)
    hot = (iota((128, count), 0) == owners).astype(F32)
    rank = jnp.sum(dot(hot.astype(BF16), earlier) * hot, axis=0, keepdims=True)
    return hot, rank.astype(jnp.int32)


def position(device, sizes):
    size_gx, size_gy = sizes
    return device % size_gy * size_gx + device // size_gy


def route_kernel(sizes, capacity, size_y, member_row, low, slot_row, hot_rows, hot_sides):
    columns = member_row.shape[1]
    size_x = columns // size_y
    earlier = (iota((128, 128), 0) < iota((128, 128), 1)).astype(F32).astype(BF16)
    seen = jnp.zeros((128, 1), F32)
    for b in range(columns // 128):
        part = slice(b * 128, (b + 1) * 128)
        members = position(member_row[:, part], sizes)
        hot = (iota((128, 128), 0) == members).astype(F32)
        count = dot(hot.astype(BF16), earlier) + seen
        rank = jnp.sum(count * hot, axis=0, keepdims=True).astype(jnp.int32)
        slot_row[:, part] = members * capacity + rank
        seen = seen + jnp.sum(hot, axis=1, keepdims=True)
    step = 256
    slots = slot_row[...]
    for b in range(hot_rows.shape[0] // step):
        hot = iota((step, columns), 0) + b * step == slots
        hot_rows[b * step : (b + 1) * step, :] = hot.astype(F32).astype(BF16)
    lane = iota((columns, 128), 1)
    place = (lane % size_x) * size_y + (lane // size_x) * (size_y - 1)
    choose = ((iota((columns, 128), 0) == place) & (lane < 2 * size_x)).astype(F32).astype(BF16)
    row = iota((8, columns), 0)
    both = jnp.where(row == 0, slots // capacity, jnp.where(row == 1, slots % capacity, 0))
    both = dot(both.astype(F32).astype(BF16), choose).astype(jnp.int32)
    side = both[0:1, :] * capacity + both[1:2, :]
    side = jnp.where(iota((1, 128), 1) < 2 * size_x, side, -1)
    for b in range(hot_sides.shape[0] // step):
        hot = iota((step, 128), 0) + b * step == side
        hot_sides[b * step : (b + 1) * step, :] = hot.astype(F32).astype(BF16)


def add_before_after(advanced, partial, x_before, x_after):
    size_x, _, _ = partial.shape
    advanced[...] = partial[...]
    half = 0.5 * STEP_DT
    advanced[0] = advanced[0] + half * smooth_rows(x_before[...])
    advanced[size_x - 1] = advanced[size_x - 1] + half * smooth_rows(x_after[...])


def inner_kernel(partial, x_before, x_after, hot_rows, send, sides, advanced):
    size_x, size_y, features = partial.shape
    add_before_after(advanced, partial, x_before, x_after)
    for i, y in enumerate((0, size_y - 1)):
        sides[i * size_x : (i + 1) * size_x, :] = advanced[:, y, :]
        advanced[:, y, :] = jnp.zeros((size_x, features), F32)
    columns = advanced[...].reshape(size_x * size_y, features).astype(BF16)
    step = 256
    for b in range(send.shape[0] // step):
        part = slice(b * step, (b + 1) * step)
        send[part, :] = dot(hot_rows[part, :], columns).astype(BF16)


def pack_kernel(inner, sides, y_before, y_after, hot_sides, members, send):
    half = 0.5 * STEP_DT
    size, features = y_before.shape
    columns = jnp.concatenate(
        [
            sides[0:size, :] + half * y_before[...],
            sides[size : 2 * size, :] + half * y_after[...],
            jnp.zeros((128 - 2 * size, features), F32),
        ],
        axis=0,
    ).astype(BF16)
    step = 512
    for b in range(send.shape[0] // step):
        part = slice(b * step, (b + 1) * step)
        send[part, :] = inner[part, :] + dot(hot_sides[part, :], columns).astype(BF16)


def as_column(row):
    wide = jnp.where(iota((128, 128), 0) == iota((128, 128), 1), row, 0)
    return jnp.sum(wide, axis=1, keepdims=True)


def prepare_kernel(capacity, size_y, element_row, weight, slot_row, sides, members, ranks, tiled):
    count = element_row.shape[1]
    lane = iota((count, 128), 1)
    for c in range(8):
        part = weight[:, (c // 4) * 128 : (c // 4 + 1) * 128]
        low = jnp.where(lane // 16 == 2 * c % 8, part, 0.0)
        high = jnp.where(lane // 16 == 2 * c % 8 + 1, part, 0.0)
        for distance in (64, 32, 16):
            low = low + pltpu.roll(low, distance, 1)
            high = high + pltpu.roll(high, distance, 1)
        tiled[c] = jnp.where(lane < 64, low, high)

    columns = slot_row.shape[1]
    elements_y = size_y // 4
    table = []
    for b in range(columns // 128):
        slots = as_column(slot_row[:, b * 128 : (b + 1) * 128])
        column = iota((128, 128), 0) + b * 128
        here = column // size_y % 4 * 4 + column % 4 == lane
        member = jnp.where(here, slots // capacity, 0).astype(F32)
        rank = jnp.where(here, slots % capacity, 0).astype(F32)
        table.append(jnp.concatenate([member, rank], axis=1).astype(BF16))
    column = iota((128, columns), 1)
    element = column // (4 * size_y) * elements_y + column % size_y // 4
    hot = (iota((128, columns), 0) == element).astype(F32).astype(BF16)
    by_element = dot(hot, jnp.concatenate(table, axis=0)).astype(BF16)
    hot = (lane == as_column(element_row[...])).astype(F32).astype(BF16)
    both = dot(hot, by_element)
    members[...] = both[:, :128].astype(jnp.int32)
    ranks[...] = both[:, 128:].astype(jnp.int32)


def silu_of_half(half):
    return half + half * jnp.tanh(half)


def first_kernel(sizes, rows, w_in, b_in, owner_row, block_row, out, blocks, w_half):
    owners = position(owner_row[...], sizes)
    hot, rank = owner_ranks(owners)
    values = block_row[...].astype(F32)
    lane = iota(blocks.shape, 1)
    first = jnp.sum(jnp.where(rank == 0, hot, 0.0) * values, axis=1, keepdims=True)
    second = jnp.sum(jnp.where(rank == 1, hot, 0.0) * values, axis=1, keepdims=True)
    blocks[...] = jnp.where(lane == 0, first, jnp.where(lane == 1, second, 0.0))

    w_half[...] = w_in[0] * jnp.asarray(0.5, BF16)
    b_half = 0.5 * b_in[...]
    step = 512
    for b in range(rows.shape[0] // step):
        part = slice(b * step, (b + 1) * step)
        out[part, :] = silu_of_half(dot(rows[part, :], w_half[...]) + b_half).astype(BF16)


def message_parts():
    return [((8 * h + q) * 128, 2 * q, 128 * h) for h in range(2) for q in range(8)]


def dot_by_output(a, b):
    return lax.dot_general(a, b, (((1,), (1,)), ((), ())), preferred_element_type=F32)


def second_kernel(first, w_mid, b_mid, w_last, blocks, out, w_half, w_flux):
    step = 512
    sources = step // 16
    lane = iota((step, 128), 1)
    own = lane // 8 == iota((step, 128), 0) % 16
    line = iota((sources, 2, 128), 1)
    w_half[...] = w_mid[0] * jnp.asarray(0.5, BF16)
    w_flux[...] = jnp.concatenate([w_last[0, 256:264, :].astype(F32)] * 16).astype(BF16)
    b_half = 0.5 * b_mid[...]
    for b in range(first.shape[0] // step):
        hidden = dot(first[b * step : (b + 1) * step, :], w_half[...])
        hidden = silu_of_half(hidden + b_half).astype(BF16)
        tends = dot_by_output(hidden, w_last[0, 0:256, :]).reshape(sources, 16, 256)
        part = slice(b * sources, (b + 1) * sources)
        for place, slot, feature in message_parts():
            out[part, :, place : place + 128] = tends[
                :, slot : slot + 2, feature : feature + 128
            ].astype(BF16)
        flux = jnp.where(own, dot_by_output(hidden, w_flux[...]), 0.0)
        flux = jnp.sum(flux.reshape(sources, 16, 128), axis=1, keepdims=True)
        names = blocks[part, :].reshape(sources, 1, 128)
        tail = jnp.where(line == 0, flux, jnp.where(line == 1, names, 0.0))
        out[part, :, 2048:2176] = tail.astype(BF16)


def contribution_kernel(sizes, answer, members, ranks, tiled, owner_row, send):
    flux = answer[:, :, 2048:2176].astype(F32)[:, 0, :].astype(BF16)
    spread = (iota((128, 128), 0) % 8 == iota((128, 128), 1) // 16).astype(F32).astype(BF16)
    lane = iota((128, 128), 1)
    group = lane // 8
    owners = position(owner_row[...], sizes)
    _, rank = owner_ranks(owners)
    hot = (iota(send.shape, 0) == owners * 2 + rank).astype(F32).astype(BF16)
    total = None
    for c in range(16):
        if c % 2 == 0:
            pair = tiled[c // 2]
            swapped = pltpu.roll(pair, 64, 1)
        weights = jnp.where(lane < 64, *((pair, swapped) if c % 2 == 0 else (swapped, pair)))
        pick = (lane == members[:, c : c + 1]).astype(F32).astype(BF16)
        value = jnp.where(group == ranks[:, c : c + 1], dot(pick, flux), 0.0)
        term = dot(value.astype(BF16), spread) * weights
        total = term if total is None else total + term
    send[...] = dot_parts(hot, total)


def columns_kernel(
    answer,
    slot_row,
    partial,
    x_before,
    x_after,
    y_before,
    y_after,
    new_state,
    sums,
    rows,
    wide,
    advanced,
):
    sources = answer.shape[0]
    slots = sources * 16
    size_x, size_y, features = partial.shape
    add_before_after(advanced, partial, x_before, x_after)
    half = 0.5 * STEP_DT
    advanced[:, 0, :] = advanced[:, 0, :] + half * y_before[...]
    advanced[:, size_y - 1, :] = advanced[:, size_y - 1, :] + half * y_after[...]
    for place, slot, feature in message_parts():
        wide[:, slot : slot + 2, feature : feature + 128] = answer[
            :, :, place : place + 128
        ].astype(F32)
    rows[...] = wide[...].reshape(slots, features).astype(BF16)
    step = 128
    lines = step // size_y
    for b in range(size_x // lines):
        hot = iota((step, slots), 1) == as_column(slot_row[:, b * step : (b + 1) * step])
        tends = dot(hot.astype(F32).astype(BF16), rows[...])
        part = slice(b * lines, (b + 1) * lines)
        new_state[part] = advanced[part] + tends.reshape(lines, size_y, features)
    names = answer[:, :, 2048:2176].astype(F32)[:, 1, :]
    lane = iota((sources, 128), 1)
    for j in range(2):
        hot = (names[:, j : j + 1].astype(jnp.int32) == lane).astype(F32)
        sums[j] = jnp.transpose(hot)[:OB_DEV, :]


def ocean_kernel(received, sums, out):
    out[...] = dot(sums[0], received[:, 0, :], HIGHEST) + dot(sums[1], received[:, 1, :], HIGHEST)


def call(kernel, outs, *args, flops=0, nbytes=0, transcendentals=0, scratch=(), limit=16, spaces=None, out_spaces=None):
    return pl.pallas_call(
        kernel,
        out_shape=[jax.ShapeDtypeStruct(s, d) for s, d in outs],
        in_specs=[
            pl.BlockSpec(memory_space=(spaces or {}).get(i, pltpu.VMEM)) for i in range(len(args))
        ],
        out_specs=[
            pl.BlockSpec(memory_space=(out_spaces or {}).get(i, pltpu.VMEM))
            for i in range(len(outs))
        ],
        scratch_shapes=list(scratch),
        compiler_params=pltpu.CompilerParams(vmem_limit_bytes=limit * MIB),
        cost_estimate=pl.CostEstimate(
            flops=flops, bytes_accessed=nbytes, transcendentals=transcendentals
        ),
    )(*args)


def shift(value, axis, step):
    size = lax.axis_size(axis)
    return lax.ppermute(value, axis, [(i, (i + step) % size) for i in range(size)])


def exchange(value):
    return lax.all_to_all(value, AXES, split_axis=0, concat_axis=0, tiled=True)


def shards(
    state,
    group_member,
    w_in,
    bias_in,
    w_mid,
    bias_mid,
    w_out,
    intersection_element,
    ocean_owner,
    ocean_block,
    regrid_weight,
):
    size_x, size_y, features = state.shape
    sizes = lax.axis_size("gx"), lax.axis_size("gy")
    devices = sizes[0] * sizes[1]
    columns = size_x * size_y
    capacity = 2 * columns // devices
    slots = devices * capacity
    count = intersection_element.shape[0]
    line = ((size_x, features), F32)

    x_low, x_high, y_low, y_high = call(
        edges_kernel,
        [line] * 4,
        state,
        nbytes=2 * MIB,
        flops=MIB,
    )
    x_before, x_after = shift(x_high, "gx", 1), shift(x_low, "gx", -1)

    def local(token):
        return call(
            local_kernel,
            [(state.shape, F32)],
            state,
            token,
            nbytes=8 * MIB,
            flops=64 * MIB,
            spaces={1: pl.ANY},
            scratch=[pltpu.VMEM((size_x + 2, size_y, features), F32)],
        )[0]

    partial = local(x_low)
    low, high = call(
        sides_kernel,
        [line] * 2,
        y_low,
        y_high,
        x_before,
        x_after,
        partial,
        spaces={4: pl.ANY},
    )
    y_before, y_after = shift(high, "gy", 1), shift(low, "gy", -1)
    slot_row, hot_rows, hot_sides = call(
        lambda *refs: route_kernel(sizes, capacity, size_y, *refs),
        [((1, columns), jnp.int32), ((slots, columns), BF16), ((slots, 128), BF16)],
        group_member.reshape(1, columns),
        low,
        spaces={1: pl.ANY},
        nbytes=8 * MIB,
        flops=64 * MIB,
    )
    inner, sides = call(
        inner_kernel,
        [((slots, features), BF16), ((2 * size_x, features), F32)],
        partial,
        x_before,
        x_after,
        hot_rows,
        nbytes=8 * MIB,
        flops=2 * slots * columns * features,
        scratch=[pltpu.VMEM(state.shape, F32)],
    )
    members, ranks, tiled = call(
        lambda *refs: prepare_kernel(capacity, size_y, *refs),
        [((count, 128), jnp.int32)] * 2 + [((8, count, 128), F32)],
        intersection_element.reshape(1, count),
        regrid_weight,
        slot_row,
        sides,
        spaces={3: pl.ANY},
        nbytes=12 * MIB,
        flops=2 * 16 * count * columns * 256,
    )
    (send,) = call(
        pack_kernel,
        [((slots, features), BF16)],
        inner,
        sides,
        y_before,
        y_after,
        hot_sides,
        members,
        nbytes=4 * MIB,
        flops=2 * slots * 128 * features,
        spaces={5: pl.ANY},
    )
    received = exchange(send.reshape(devices, capacity, features)).reshape(slots, features)

    hidden = w_in.shape[2]
    owner_row = ocean_owner.reshape(1, count)
    first, blocks = call(
        lambda *refs: first_kernel(sizes, *refs),
        [((slots, hidden), BF16), ((devices, 128), F32)],
        received,
        w_in,
        bias_in,
        owner_row,
        ocean_block.reshape(1, count),
        nbytes=6 * MIB,
        flops=2 * slots * features * hidden,
        transcendentals=slots * hidden,
        scratch=[pltpu.VMEM((features, hidden), BF16)],
    )
    (answered,) = call(
        second_kernel,
        [((devices, 2, 2176), BF16)],
        first,
        w_mid,
        bias_mid,
        jnp.swapaxes(w_out, 1, 2),
        blocks,
        nbytes=8 * MIB,
        flops=2 * slots * hidden * (hidden + 384),
        transcendentals=slots * hidden,
        limit=24,
        scratch=[pltpu.VMEM((hidden, hidden), BF16), pltpu.VMEM((128, hidden), BF16)],
    )
    answer = exchange(answered)
    (ocean_send,) = call(
        lambda *refs: contribution_kernel(sizes, *refs),
        [((2 * devices, 128), F32)],
        answer,
        members,
        ranks,
        tiled,
        owner_row,
        nbytes=4 * MIB,
        flops=2 * 2 * 2048 * 128 * 128,
    )
    ocean_got = exchange(ocean_send.reshape(devices, 2, 128))
    partial = local(ocean_send)
    new_state, sums = call(
        columns_kernel,
        [(state.shape, F32), ((2, OB_DEV, devices), F32)],
        answer,
        slot_row,
        partial,
        x_before,
        x_after,
        y_before,
        y_after,
        nbytes=12 * MIB,
        flops=2 * slots * columns * features,
        scratch=[
            pltpu.VMEM((slots, features), BF16),
            pltpu.VMEM((devices, 16, features), F32),
            pltpu.VMEM(state.shape, F32),
        ],
    )
    (ocean_total,) = call(
        ocean_kernel, [((OB_DEV, 128), F32)], ocean_got, sums, nbytes=MIB, flops=MIB
    )
    return (new_state, ocean_total)


def solution(mesh):
    return jax.shard_map(
        shards,
        mesh=mesh,
        in_specs=(
            P("gx", "gy", None),
            P(("gx", "gy"), None),
            P(("gx", "gy"), None, None),
            P(("gx", "gy"), None),
            P(("gx", "gy"), None, None),
            P(("gx", "gy"), None),
            P(("gx", "gy"), None, None),
            P(("gx", "gy")),
            P(("gx", "gy"), None),
            P(("gx", "gy")),
            P(("gx", "gy"), None),
        ),
        out_specs=(P("gx", "gy", None), P(("gx", "gy"), None)),
        check_vma=False,
    )
```
